128 devices in a mesh: grp: 4 (over z_lo, core), lon: 32 (over x, y, z_hi).
Axes of the slice: x: 4, y: 4, z: 4 (z_hi: 2, z_lo: 2; z = z_hi * 2 + z_lo), core: 2. Of those that a mesh axis runs over, the one named last changes fastest.
Arguments:
- field: float32 [16, 1024, 128], P('grp', 'lon'), may hold values from -6 to 6
- wind: float32 [16, 1024, 128], P('grp', 'lon'), may hold values from -1 to 1
- w_in: bfloat16 [128, 2048], replicated, may hold values from -0.5 to 0.5
- w_mid: bfloat16 [2048, 2048], replicated, may hold values from -0.125 to 0.125
- w_out: bfloat16 [2048, 128], replicated, may hold values from -0.125 to 0.125
- targets: float32 [4096, 128], P('lon'), may hold values from -6 to 6
- column_map: int32 [4, 32, 128, 1], P('grp', 'lon'), may hold values from 0 to 31; in each aligned block of 128 rows (0 to 127, 128 to 255, ..., all dimensions but the last counted through in order) at most 8 rows name the same one
- batch_count: int32 [32], replicated, may hold values from 1 to 128, 2048 in all
Outputs:
- field_out: float32 [16, 1024, 128], P('grp', 'lon')
- grad_mid: float32 [2048, 2048], P(('grp', 'lon'))
- grad_out: float32 [2048, 128], P(('grp', 'lon'))
The draws below stay inside these ranges and needn't reach their ends.
Inputs may be any that keep to these rules, and one draw needn't show every extreme that they name: `column_map`: among the 128 columns of one device in the first 3 bands at most 8 name one trainer, and that bound is reached. The last band's entries are not read. `batch_count`: the largest entry equals 128.
All inputs are finite; a program needn't handle non-finite values.
Results may differ from the reference program's by a relative error of at most 0.0034.
Values may be sent and summed in bfloat16 or wider, within the bound.
A program may use at most 128 MiB of HBM per device.

```python
import math
import jax
import jax.numpy as jnp
import numpy as np
from jax import lax

LEV = 128
HID = 2048
STEPS = 2
LAT_DEV = 4
LON_DEV = 32
COLS = 128
CAP = 8
LAT = 16
LON = 1024
ROWS = 4096
N_GRP = 4
N_LON = 32


def block_scale(stream_key, dims, cuts, low, largest):
    def one(axis_at, blocks):
        heights = jax.random.uniform(jax.random.fold_in(jax.random.fold_in(stream_key, 6), axis_at), (blocks,), jnp.float32, low / len(cuts), largest / len(cuts))
        return jnp.repeat(jnp.exp(heights), dims[axis_at] // blocks).reshape((-1,) + (1,) * (len(dims) - axis_at - 1))

    factor_of = one(*cuts[0])
    for cut in cuts[1:]:
        factor_of = factor_of * one(*cut)
    return factor_of


def length_profile(amount, total, limit, skew):
    portions = [(1 << 20) // math.isqrt(grade ** skew) + 1 for grade in range(2, amount + 1)]
    spare, holding = total - limit - (amount - 1), [1] * (amount - 1)
    while spare > 0:
        free = [i for i in range(amount - 1) if holding[i] < limit]
        mass, left = sum([portions[i] for i in free]), spare
        for i in free:
            more = min(limit - holding[i], max(1, left * portions[i] // mass), spare)
            holding[i] = holding[i] + more
            spare = spare - more
    return np.array([limit] + holding)


def uneven_parts(key, amount, total, most, slope):
    if amount == 2:
        one = jax.random.randint(key, (), max(1, total - most), min(most, total - 1) + 1)
        return jnp.stack([one, total - one])
    tallies = jnp.asarray(length_profile(amount, total, most, slope), jnp.int32)
    pairs = (amount - 1) // 2
    source_of, sink = tallies[1:1 + 2 * pairs:2], tallies[2:2 + 2 * pairs:2]
    room = jnp.minimum(source_of - 1, most - sink)
    passed = jax.random.randint(jax.random.fold_in(key, 1), (pairs,), 0, 1 << 20) % (room + 1)
    tallies = tallies.at[1:1 + 2 * pairs:2].set(source_of - passed).at[2:2 + 2 * pairs:2].set(sink + passed)
    return tallies[jax.random.permutation(jax.random.fold_in(key, 2), amount)]


def deal_out(own_key, own, number, rows, amount, top, most, skew):
    order = jax.random.permutation(own_key, amount)
    packed, ordinary = load_shares(amount, rows * top, most, skew, True), load_shares(amount, rows * top, most, skew, False)
    places = jnp.arange(amount)

    def named(sizes, rotation):
        used = int((sizes > 0).sum())
        fixed = max(1, used // 4)
        moved = fixed + (places - fixed + rotation * (used - fixed)) % max(1, amount - fixed)
        return jnp.zeros((amount,), jnp.int32).at[order[jnp.where(places < fixed, places, moved)]].set(jnp.asarray(sizes, jnp.int32))

    sizes = jnp.where(number % 4 == 0, named(packed, number // 4), named(ordinary, number - number // 4 - 1))
    mixed = jax.random.permutation(jax.random.fold_in(own, 3), amount)
    source_of, receiver = mixed[0:amount // 2 * 2:2], mixed[1:amount // 2 * 2:2]
    slack = jnp.minimum(sizes[source_of] - 1, most - sizes[receiver]) // 2
    slack = jnp.where((source_of == order[0]) | (receiver == order[0]) | (sizes[receiver] == 0), 0, jnp.maximum(slack, 0))
    moved = jax.random.randint(jax.random.fold_in(own, 4), (amount // 2,), 0, 1 << 20) % (slack + 1)
    sizes = sizes.at[source_of].add(-moved).at[receiver].add(moved)
    members = jnp.searchsorted(jnp.cumsum(sizes), jnp.arange(rows * top), side="right").astype(jnp.int32)
    table = members.reshape(top, rows).T
    table = table[jax.random.permutation(jax.random.fold_in(own, 1), rows)]
    rotation = jax.random.randint(jax.random.fold_in(own, 2), (rows, 1), 0, top)
    return jnp.take_along_axis(table, (jnp.arange(top)[None, :] + rotation) % top, axis=1)


def load_shares(amount, total, bound, lean, full):
    weights = [(1 << 20) // math.isqrt(rank ** lean) + 1 for rank in range(1, amount + 1)]
    largest = bound if full else min(bound, max(-(-total // amount), total * weights[0] // sum(weights)))
    least = 1 if total - largest >= amount - 1 else 0
    given, spare = [largest] + [least] * (amount - 1), total - largest - least * (amount - 1)
    while spare > 0:
        candidates = [i for i in range(1, amount) if given[i] < largest] or [i for i in range(1, amount) if given[i] < bound]
        mass, remaining = sum([weights[i] for i in candidates]), spare
        for i in candidates:
            more = min(bound - given[i], max(1, remaining * weights[i] // mass), spare)
            given[i] = given[i] + more
            spare = spare - more
    return np.array(given)


def normal_values(rng, dims, width, reach, cuts=(), kind=jnp.bfloat16):
    entries = width * jax.random.normal(rng, dims, jnp.float32)
    if cuts:
        entries = entries * block_scale(rng, dims, cuts, -0.22, 0.18)
    return jnp.clip(entries, -reach, reach).astype(kind)


def setup_inputs(seed: int = 0) -> dict:
    streams_of = jax.random.split(jax.random.key(seed), 9)
    field = normal_values(streams_of[0], (LAT, LON, LEV), 1.0, 6.0, ((0, 4), (1, 32)), jnp.float32)
    wind = jnp.clip(jax.random.uniform(streams_of[1], (LAT, LON, LEV), jnp.float32, -1.0, 1.0) * block_scale(streams_of[1], (LAT, LON, LEV), ((0, 4), (1, 32)), -0.4, 0.0), -1.0, 1.0)
    w_in = normal_values(streams_of[2], (LEV, HID), LEV ** -0.5, 0.5)
    w_mid = normal_values(streams_of[3], (HID, HID), HID ** -0.5, 0.125)
    w_out = normal_values(streams_of[4], (HID, LEV), HID ** -0.5, 0.125)
    targets = normal_values(streams_of[5], (ROWS, LEV), 1.0, 6.0, ((0, 32),), jnp.float32)
    column_map_keys = jax.random.split(jax.random.fold_in(streams_of[6], 1), N_GRP * N_LON * COLS // COLS)
    column_map_turns = jax.random.permutation(jax.random.fold_in(streams_of[6], 3), N_GRP * N_LON * COLS // COLS)
    column_map = jax.vmap(lambda own, number: deal_out(jax.random.fold_in(streams_of[6], 2), own, number, COLS, N_LON, 1, CAP, 2))(column_map_keys, column_map_turns).reshape((N_GRP, N_LON, COLS, 1))
    batch_count = uneven_parts(streams_of[7], N_LON, N_LON * COLS // 2, COLS, 2).astype(jnp.int32)
    return {"field": field, "wind": wind, "w_in": w_in, "w_mid": w_mid, "w_out": w_out, "targets": targets, "column_map": column_map, "batch_count": batch_count}


loss_scale = 1024.0
physics_share = 0.5


def silu_slope(values):
    sig = jax.nn.sigmoid(values)
    return sig * (1.0 + values * (1.0 - sig))


def network_pass(inputs, wanted, weights, w_in, w_mid, w_out):
    first_pre = jnp.dot(inputs, w_in, preferred_element_type=jnp.float32)
    first_act = jax.nn.silu(first_pre).astype(jnp.bfloat16)
    second_pre = jnp.dot(first_act, w_mid, preferred_element_type=jnp.float32)
    second_act = jax.nn.silu(second_pre).astype(jnp.bfloat16)
    predicted = jnp.dot(second_act, w_out, preferred_element_type=jnp.float32)
    out_slope = ((predicted - wanted) * weights[:, None]).astype(jnp.bfloat16)
    back_hidden = lax.dot_general(out_slope, w_out, (((1,), (1,)), ((), ())), preferred_element_type=jnp.float32)
    mid_slope = (back_hidden * silu_slope(second_pre)).astype(jnp.bfloat16)
    return predicted, first_act, second_act, out_slope, mid_slope


def advance(current, wind_band):
    padded = jnp.pad(current, ((1, 1), (0, 0), (0, 0)))
    northern = padded[2:]
    southern = padded[:-2]
    eastern = jnp.roll(current, -1, axis=1)
    western = jnp.roll(current, 1, axis=1)
    return current - 0.25 * wind_band * (eastern - western) + 0.15 * (eastern + western + northern + southern - 4.0 * current)


def to_columns(values, bands):
    shaped = values.reshape(bands, LAT_DEV, N_LON, LON_DEV, values.shape[-1]).transpose(0, 2, 1, 3, 4)
    return shaped.reshape(bands * N_LON * COLS, values.shape[-1])


def from_columns(row_block, bands):
    shaped = row_block.reshape(bands, N_LON, LAT_DEV, LON_DEV, row_block.shape[-1]).transpose(0, 2, 1, 3, 4)
    return shaped.reshape(bands * LAT_DEV, N_LON * LON_DEV, row_block.shape[-1])


def reference(field, wind, w_in, w_mid, w_out, targets, column_map, batch_count):
    sim_bands = N_GRP - 1
    sim_rows = sim_bands * LAT_DEV
    start = field[:sim_rows]
    wind_band = wind[:sim_rows]
    current = start
    for iteration in range(STEPS):
        current = advance(current, wind_band)
    increment = (current - start).astype(jnp.bfloat16)
    sent_inputs = to_columns(start.astype(jnp.bfloat16), sim_bands)
    sent_goals = to_columns(increment, sim_bands).astype(jnp.float32)
    replay = to_columns(field[sim_rows:], 1).astype(jnp.bfloat16)
    inputs = jnp.concatenate([sent_inputs, replay], 0)
    wanted = jnp.concatenate([sent_goals, targets], 0)
    trainer_of = column_map[:sim_bands].reshape(-1)
    loads = jnp.sum((trainer_of[:, None] == jnp.arange(N_LON)[None, :]).astype(jnp.float32), 0)
    row_total = batch_count.astype(jnp.float32) + loads
    loss_weight = loss_scale / (N_LON * row_total)
    replay_index = jnp.arange(N_LON * COLS)
    owner = replay_index // COLS
    in_batch = (replay_index % COLS < batch_count[owner]).astype(jnp.float32)
    weights = jnp.concatenate([loss_weight[trainer_of], in_batch * loss_weight[owner]], 0)
    predicted, first_act, second_act, out_slope, mid_slope = network_pass(inputs, wanted, weights, w_in, w_mid, w_out)
    grad_mid = jnp.dot(first_act.T, mid_slope, preferred_element_type=jnp.float32)
    grad_out = jnp.dot(second_act.T, out_slope, preferred_element_type=jnp.float32)
    sim_count = sim_bands * N_LON * COLS
    tendency = lax.optimization_barrier(predicted[:sim_count].astype(jnp.bfloat16)).astype(jnp.float32)
    sim_out = current + physics_share * from_columns(tendency, sim_bands)
    replay_out = from_columns(predicted[sim_count:], 1)
    field_out = jnp.concatenate([sim_out, replay_out], 0)
    return field_out, grad_mid, grad_out
```

```python
import jax
import jax.numpy as jnp
from jax import lax
from jax.sharding import PartitionSpec as P

STEPS = 2


loss_scale = 1024.0
physics_share = 0.5


def padded_2(cells, sides, width):
    for axis, dim in sides:
        count = lax.axis_size(axis)
        head = lax.slice_in_dim(cells, 0, width, axis=dim)
        tail = lax.slice_in_dim(cells, cells.shape[dim] - width, cells.shape[dim], axis=dim)
        cells = jnp.concatenate(
            [
                lax.ppermute(tail, axis, [(i, (i + 1) % count) for i in range(count)]),
                cells,
                lax.ppermute(head, axis, [((i + 1) % count, i) for i in range(count)]),
            ],
            axis=dim,
        )
    return cells


def silu_slope(values):
    sig = jax.nn.sigmoid(values)
    return sig * (1.0 + values * (1.0 - sig))


def network_pass(inputs, wanted, weights, w_in, w_mid, w_out):
    first_pre = jnp.dot(inputs, w_in, preferred_element_type=jnp.float32)
    first_act = jax.nn.silu(first_pre).astype(jnp.bfloat16)
    second_pre = jnp.dot(first_act, w_mid, preferred_element_type=jnp.float32)
    second_act = jax.nn.silu(second_pre).astype(jnp.bfloat16)
    predicted = jnp.dot(second_act, w_out, preferred_element_type=jnp.float32)
    out_slope = ((predicted - wanted) * weights[:, None]).astype(jnp.bfloat16)
    back_hidden = lax.dot_general(
        out_slope, w_out, (((1,), (1,)), ((), ())), preferred_element_type=jnp.float32
    )
    mid_slope = (back_hidden * silu_slope(second_pre)).astype(jnp.bfloat16)
    return (predicted, first_act, second_act, out_slope, mid_slope)


def stencil(padded, wind_band):
    center = padded[1:-1, 1:-1]
    eastern = padded[1:-1, 2:]
    western = padded[1:-1, :-2]
    northern = padded[2:, 1:-1]
    southern = padded[:-2, 1:-1]
    return (
        center
        - 0.25 * wind_band * (eastern - western)
        + 0.15 * (eastern + western + northern + southern - 4.0 * center)
    )


def body(field, wind, w_in, w_mid, w_out, targets, column_map, batch_count):
    group_index = lax.axis_index("grp")
    lon_index = lax.axis_index("lon")
    n_grp = lax.axis_size("grp")
    n_lon = lax.axis_size("lon")
    lat_rows, lon_cells, levels = field.shape
    columns = lat_rows * lon_cells
    hidden = w_mid.shape[0]
    is_trainer = group_index == n_grp - 1
    low_edge = group_index == 0
    high_edge = group_index == n_grp - 2
    current = field
    for iteration in range(STEPS):
        padded = padded_2(current, (("grp", 0), ("lon", 1)), 1)
        row_ids = jnp.arange(padded.shape[0])
        outside = (row_ids < 1) & low_edge | (row_ids >= padded.shape[0] - 1) & high_edge
        current = stencil(jnp.where(outside[:, None, None], 0.0, padded), wind)
    trainer_of = column_map.reshape(columns)
    matches = (trainer_of[:, None] == jnp.arange(n_lon)[None, :]).astype(jnp.float32)
    loads = lax.psum(jnp.where(is_trainer, 0.0, jnp.sum(matches, 0)), ("grp", "lon"))
    trainer_weight = loss_scale / (n_lon * (batch_count.astype(jnp.float32) + loads))
    column_weight = jnp.sum(matches * trainer_weight[None, :], 1)
    batch_rows = lax.dynamic_index_in_dim(batch_count, lon_index, 0, keepdims=False)
    own_weight = lax.dynamic_index_in_dim(trainer_weight, lon_index, 0, keepdims=False)
    replay_weight = jnp.where(jnp.arange(columns) < batch_rows, own_weight, 0.0)
    weights = jnp.where(is_trainer, replay_weight, column_weight)
    inputs = field.reshape(columns, levels).astype(jnp.bfloat16)
    increment = (current - field).reshape(columns, levels).astype(jnp.bfloat16)
    wanted = jnp.where(is_trainer, targets, increment.astype(jnp.float32))
    predicted, first_act, second_act, out_slope, mid_slope = network_pass(
        inputs, wanted, weights, w_in, w_mid, w_out
    )
    tendency = lax.reduce_precision(predicted, 8, 7)
    sim_out = current + physics_share * tendency.reshape(lat_rows, lon_cells, levels)
    field_out = jnp.where(is_trainer, predicted.reshape(lat_rows, lon_cells, levels), sim_out)
    part_mid = lax.dot_general(
        first_act, mid_slope, (((0,), (0,)), ((), ())), preferred_element_type=jnp.float32
    )
    part_out = lax.dot_general(
        second_act, out_slope, (((0,), (0,)), ((), ())), preferred_element_type=jnp.float32
    )
    summed = lax.psum_scatter(
        jnp.concatenate([part_mid, part_out], 1), ("grp", "lon"), scatter_dimension=0, tiled=True
    )
    return (field_out, summed[:, :hidden], summed[:, hidden:])


def solution(mesh):
    placed = (
        P("grp", "lon", None),
        P("grp", "lon", None),
        P(),
        P(),
        P(),
        P("lon", None),
        P("grp", "lon", None, None),
        P(),
    )
    return jax.shard_map(
        body,
        mesh=mesh,
        in_specs=placed,
        out_specs=(P("grp", "lon", None), P(("grp", "lon"), None), P(("grp", "lon"), None)),
        check_vma=False,
    )
```

```python
import jax
import jax.numpy as jnp
from jax import lax
from jax.experimental import pallas as pl
from jax.experimental.pallas import tpu as pltpu
from jax.sharding import PartitionSpec as P

MESH = pl.DeviceIdType.MESH
bf16, f32 = jnp.bfloat16, jnp.float32

LOSS_SCALE = 1024.0
PHYSICS_SHARE = 0.5
RANKS = 8
SIDE = 4
LANES = 128
BLOCK = 256
NT = (((1,), (1,)), ((), ()))
TN = (((0,), (0,)), ((), ()))


def sigmoid(v):
    return 0.5 + 0.5 * jnp.tanh(0.5 * v)


def wide(i, size):
    return pl.ds(pl.multiple_of(i * size, size), size)


def kernel(
    field, wind, w_in, w_mid, w_out, targets, cmap, batch,
    field_out, grad_mid, grad_out,
    ext, gust, mids, win, wint, wout, goal, first, firsts, second, slope, pred, inputs,
    step, outgoing, mine, cnt_out, cnt_in, sum_out, sum_in,
    part, got_x, got_y, half, got_h, final, got_f,
    load_sem, mid_sem, halo_s, halo_r, in_s, in_r, cnt_s, cnt_r, sum_s, sum_r,
    m_s, m_r, one_s, one_r, two_s, two_r, fin_s, fin_r,
):
    grp, lon = lax.axis_index("grp"), lax.axis_index("lon")
    place, zh = lax.div(lon, 2), lax.rem(lon, 2)
    x, y = lax.div(place, SIDE), lax.rem(place, SIDE)
    rank = zh * 4 + grp
    is_trainer = grp == 3

    def rank_at(k):
        return lax.rem(rank + k, RANKS)

    def ring(k):
        other = rank_at(k)
        return (lax.rem(other, 4), place * 2 + lax.div(other, 4))

    def plane(k):
        return (grp, lax.rem(place + k, SIDE * SIDE) * 2 + zh)

    def along_x(k):
        return (grp, lax.rem(x + k, SIDE) * (2 * SIDE) + y * 2 + zh)

    def along_y(k):
        return (grp, x * (2 * SIDE) + lax.rem(y + k, SIDE) * 2 + zh)

    def beside(dg, dl):
        return (lax.rem(grp + dg + 4, 4), lax.rem(lon + dl + 32, 32))

    def remote(src, dst, send, recv, to):
        return pltpu.make_async_remote_copy(
            src_ref=src, dst_ref=dst, send_sem=send, recv_sem=recv,
            device_id=to, device_id_type=MESH,
        )

    loads = [
        pltpu.make_async_copy(field, ext.at[2:6, 8:40], load_sem.at[0]),
        pltpu.make_async_copy(w_in, win, load_sem.at[1]),
        pltpu.make_async_copy(wind, gust.at[1:5, 8:40], load_sem.at[2]),
        pltpu.make_async_copy(w_out, wout, load_sem.at[3]),
        pltpu.make_async_copy(targets, goal, load_sem.at[4]),
    ]

    def mid_load(c):
        return pltpu.make_async_copy(w_mid.at[:, wide(c, BLOCK)], mids.at[c], mid_sem.at[c])

    for load in loads:
        load.start()
    for c in range(RANKS):
        mid_load(c).start()

    barrier = pltpu.get_barrier_semaphore()
    greeted = [ring(k) for k in range(1, RANKS)] + [plane(k) for k in range(1, SIDE * SIDE)]
    far = 2 * zh - 1
    greeted += [beside(dg, far) for dg in (-1, 0, 1)]
    for other in greeted:
        pl.semaphore_signal(barrier, inc=1, device_id=other, device_id_type=MESH)

    names = jnp.broadcast_to(cmap[...].astype(f32), (LANES, LANES)).T
    ids = lax.broadcasted_iota(jnp.int32, (LANES, LANES), 1).astype(f32)
    match = (names == ids).astype(f32)
    own_count = jnp.sum(match, 0, keepdims=True) * jnp.where(is_trainer, 0.0, 1.0)
    cnt_out[...] = jnp.broadcast_to(own_count, (8, LANES))

    loads[0].wait()
    own_in = ext[2:6, 8:40].reshape(LANES, LANES).astype(bf16)
    inputs[wide(rank, LANES), :] = own_in
    loads[2].wait()
    pl.semaphore_wait(barrier, len(greeted))

    in_copies = [
        remote(
            inputs.at[wide(rank, LANES)], inputs.at[wide(rank, LANES)],
            in_s.at[k], in_r.at[k], ring(k),
        ) for k in range(1, RANKS)
    ]
    cnt_copies = [
        remote(cnt_out, cnt_in.at[k], cnt_s.at[k], cnt_r.at[k], ring(k)) for k in range(1, RANKS)
    ]
    halo = [
        (ext.at[2:4, 8:40], ext.at[6:8, 8:40], -1, 0),
        (ext.at[4:6, 8:40], ext.at[0:2, 8:40], 1, 0),
        (ext.at[2:6, 8:16], ext.at[2:6, 40:48], 0, -1),
        (ext.at[2:6, 32:40], ext.at[2:6, 0:8], 0, 1),
        (ext.at[2:3, 8:16], ext.at[6:7, 40:48], -1, -1),
        (ext.at[2:3, 32:40], ext.at[6:7, 0:8], -1, 1),
        (ext.at[5:6, 8:16], ext.at[1:2, 40:48], 1, -1),
        (ext.at[5:6, 32:40], ext.at[1:2, 0:8], 1, 1),
        (gust.at[1:2, 8:40], gust.at[5:6, 8:40], -1, 0),
        (gust.at[4:5, 8:40], gust.at[0:1, 8:40], 1, 0),
        (gust.at[1:5, 8:16], gust.at[1:5, 40:48], 0, -1),
        (gust.at[1:5, 32:40], gust.at[1:5, 0:8], 0, 1),
    ]
    halo_copies = [
        remote(src, dst, halo_s.at[i], halo_r.at[i], beside(dg, dl))
        for i, (src, dst, dg, dl) in enumerate(halo)
    ]
    for copy in cnt_copies + halo_copies + in_copies:
        copy.start()

    loads[1].wait()
    own_in = inputs[wide(rank, LANES), :]

    def first_step(c, carry):
        pre = jnp.dot(own_in, win[:, wide(c, 512)], preferred_element_type=f32)
        first[:, wide(c, 512)] = (pre * sigmoid(pre)).astype(bf16)
        return carry

    lax.fori_loop(0, 4, first_step, 0)
    loads[3].wait()
    pred[...] = jnp.zeros_like(pred)

    def second_step(c, carry):
        mid_load(c).wait()
        pre = jnp.dot(first[...], mids[c], preferred_element_type=f32)
        sig = sigmoid(pre)
        act = (pre * sig).astype(bf16)
        second[:, wide(c, BLOCK)] = act
        slope[:, wide(c, BLOCK)] = sig * (1.0 + pre * (1.0 - sig))
        pred[...] += jnp.dot(act, wout[wide(c, BLOCK), :], preferred_element_type=f32)
        return carry

    lax.fori_loop(0, 4, second_step, 0)

    total = cnt_out[...]
    for k in range(1, RANKS):
        cnt_copies[k - 1].wait_recv()
        total = total + cnt_in[k]
    sum_out[...] = total
    sum_copies = [
        remote(sum_out, sum_in.at[k], sum_s.at[k], sum_r.at[k], plane(k))
        for k in range(1, SIDE * SIDE)
    ]
    for copy in sum_copies:
        copy.start()

    lax.fori_loop(4, RANKS, second_step, 0)

    for copy in halo_copies:
        copy.wait_recv()
    low, high = grp == 0, grp == 2

    def masked(row, values):
        if row < 0:
            return jnp.where(low, 0.0, values)
        if row > 3:
            return jnp.where(high, 0.0, values)
        return values

    def advanced(c, n, s, e, w, u):
        return c - 0.25 * u * (e - w) + 0.15 * (e + w + n + s - 4.0 * c)

    for row in range(-1, 5):
        i = row + 2
        c = masked(row, ext[i, 7:41])
        e, w = masked(row, ext[i, 8:42]), masked(row, ext[i, 6:40])
        n, s = masked(row + 1, ext[i + 1, 7:41]), masked(row - 1, ext[i - 1, 7:41])
        step[row + 1, 7:41] = masked(row, advanced(c, n, s, e, w, gust[row + 1, 7:41]))
    current = []
    for row in range(4):
        c = step[row + 1, 8:40]
        e, w = step[row + 1, 9:41], step[row + 1, 7:39]
        n, s = step[row + 2, 8:40], step[row, 8:40]
        current.append(advanced(c, n, s, e, w, gust[row + 1, 8:40]))
    current = jnp.concatenate(current, 0)
    start = ext[2:6, 8:40].reshape(LANES, LANES)
    increment = (current - start).astype(bf16).astype(f32)
    loads[4].wait()
    wanted = jnp.where(is_trainer, goal[...], increment)

    total = sum_out[...]
    for k in range(1, SIDE * SIDE):
        sum_copies[k - 1].wait_recv()
        total = total + sum_in[k]
    valid = batch[...].astype(f32)
    weight = LOSS_SCALE / (32.0 * (valid + total[0:1, 0:32]))
    column_weight = jnp.sum(match[:, 0:32] * weight, 1, keepdims=True)
    own = lax.broadcasted_iota(jnp.int32, (1, 32), 1) == lon
    own_weight = jnp.sum(jnp.where(own, weight, 0.0), 1, keepdims=True)
    own_valid = jnp.sum(jnp.where(own, valid, 0.0), 1, keepdims=True)
    rows = lax.broadcasted_iota(jnp.int32, (LANES, 1), 0).astype(f32)
    replay_weight = jnp.where(rows < own_valid, own_weight, 0.0)
    row_weight = jnp.where(is_trainer, replay_weight, column_weight)

    predicted = pred[...]
    tendency = predicted.astype(bf16).astype(f32)
    sim = current + PHYSICS_SHARE * tendency
    field_out[...] = jnp.where(is_trainer, predicted, sim).reshape(4, 32, LANES)
    out_slope = ((predicted - wanted) * row_weight).astype(bf16)

    def m_copy(k, h):
        return remote(
            outgoing.at[h, rank_at(k)], mine.at[h, wide(rank, LANES)],
            m_s.at[h, k], m_r.at[h, k], ring(k),
        )

    def mid_step(k, carry):
        t = rank_at(k)
        back = lax.dot_general(out_slope, wout[wide(t, BLOCK), :], NT, preferred_element_type=f32)
        value = (back * slope[:, wide(t, BLOCK)]).astype(bf16)
        outgoing[0, t] = value[:, :LANES]
        outgoing[1, t] = value[:, LANES:]

        @pl.when(k < RANKS)
        def _():
            m_copy(k, 0).start()

        return carry

    lax.fori_loop(1, RANKS + 1, mid_step, 0)
    for k in range(1, RANKS):
        m_copy(k, 1).start()
    for h in range(2):
        mine[h, wide(rank, LANES), :] = outgoing[h, rank]

    def x_copy(q, k):
        return remote(
            part.at[q, 0:2, lax.rem(x + k, SIDE)], got_x.at[q, k],
            one_s.at[q, 0, k], one_r.at[q, 0, k], along_x(k),
        )

    def y_copy(q, k):
        return remote(
            part.at[q, 2:4, :, lax.rem(y + k, SIDE)], got_y.at[q, k],
            one_s.at[q, 1, k], one_r.at[q, 1, k], along_y(k),
        )

    def x2_copy(q, k):
        return remote(
            half.at[q, 0, lax.rem(y + k, SIDE)], got_h.at[q, 0, k],
            two_s.at[q, 0, k], two_r.at[q, 0, k], along_y(k),
        )

    def y2_copy(q, k):
        return remote(
            half.at[q, 1, lax.rem(x + k, SIDE)], got_h.at[q, 1, k],
            two_s.at[q, 1, k], two_r.at[q, 1, k], along_x(k),
        )

    def fin_copy(q, k):
        if q == 0:
            dst = got_f.at[k]
        else:
            dst = grad_mid.at[:, wide(rank * 2 + (q - 1), LANES)]
        return remote(
            final.at[q, rank_at(k)], dst, fin_s.at[q, k], fin_r.at[q, k], ring(k)
        )

    def make_part(q, product):
        def rows_step(c, carry):
            value = product(c).astype(bf16).reshape(2, SIDE, 32, LANES)
            part[q, lax.div(c, 2), pl.ds(lax.rem(c, 2) * 2, 2)] = value
            return carry

        lax.fori_loop(0, 4, rows_step, 0)
        for k in range(1, SIDE):
            x_copy(q, k).start()
        lax.fori_loop(4, 8, rows_step, 0)
        for k in range(1, SIDE):
            y_copy(q, k).start()

    def reduce_one(q):
        total = part[q, 0:2, x].astype(f32)
        for k in range(1, SIDE):
            x_copy(q, k).wait_recv()
            total = total + got_x[q, k].astype(f32)
        total = total.astype(bf16)
        for g in range(2):
            half[q, 0, :, g] = total[g]
        for k in range(1, SIDE):
            x2_copy(q, k).start()
        total = part[q, 2:4, :, y].astype(f32)
        for k in range(1, SIDE):
            y_copy(q, k).wait_recv()
            total = total + got_y[q, k].astype(f32)
        total = total.astype(bf16)
        for g in range(2):
            half[q, 1, :, g] = total[g]
        for k in range(1, SIDE):
            y2_copy(q, k).start()

    def reduce_two(q):
        for axis, own_at, copies in ((0, y, x2_copy), (1, x, y2_copy)):
            total = half[q, axis, own_at].astype(f32)
            for k in range(1, SIDE):
                copies(q, k).wait_recv()
                total = total + got_h[q, axis, k].astype(f32)
            for g in range(2):
                for z in range(2):
                    final[q, z * 4 + axis * 2 + g] = total[g, z * 16 : z * 16 + 16]
        for k in range(1, RANKS):
            fin_copy(q, k).start()

    make_part(
        0,
        lambda c: lax.dot_general(
            second[:, wide(c, BLOCK)], out_slope, TN, preferred_element_type=f32
        ),
    )

    for copy in in_copies:
        copy.wait_recv()

    def turn_step(c, carry):
        wint[wide(c, BLOCK), :] = win[:, wide(c, BLOCK)].T
        return carry

    lax.fori_loop(0, RANKS, turn_step, 0)

    def firsts_step(i, carry):
        c, n = lax.div(i, 2), lax.rem(i, 2)
        pre = lax.dot_general(
            wint[wide(c, BLOCK), :], inputs[wide(n, 512), :], NT, preferred_element_type=f32
        )
        firsts[wide(c, BLOCK), wide(n, 512)] = (pre * sigmoid(pre)).astype(bf16)
        return carry

    lax.fori_loop(0, 2 * RANKS, firsts_step, 0)
    reduce_one(0)

    for h in range(2):
        for k in range(1, RANKS):
            m_copy(k, h).wait_recv()
        make_part(
            1 + h,
            lambda c: jnp.dot(firsts[wide(c, BLOCK), :], mine[h], preferred_element_type=f32),
        )
        if h == 0:
            reduce_two(0)
    reduce_one(1)
    reduce_one(2)
    reduce_two(1)
    reduce_two(2)

    total = final[0, rank]
    for k in range(1, RANKS):
        fin_copy(0, k).wait_recv()
        total = total + got_f[k]
    grad_out[...] = total
    for h in range(2):
        grad_mid[:, wide(rank * 2 + h, LANES)] = final[1 + h, rank]
    for h in range(2):
        for k in range(1, RANKS):
            fin_copy(1 + h, k).wait_recv()

    for copy in in_copies + cnt_copies + halo_copies + sum_copies:
        copy.wait_send()
    for h in range(2):
        for k in range(1, RANKS):
            m_copy(k, h).wait_send()
    for q in range(3):
        for k in range(1, SIDE):
            x_copy(q, k).wait_send()
            y_copy(q, k).wait_send()
            x2_copy(q, k).wait_send()
            y2_copy(q, k).wait_send()
        for k in range(1, RANKS):
            fin_copy(q, k).wait_send()


def body(field, wind, w_in, w_mid, w_out, targets, column_map, batch_count):
    vmem = pl.BlockSpec(memory_space=pltpu.VMEM)
    any_place = pl.BlockSpec(memory_space=pl.ANY)
    hid = w_mid.shape[0]
    dma = pltpu.SemaphoreType.DMA
    V = pltpu.VMEM
    return pl.pallas_call(
        kernel,
        out_shape=(
            jax.ShapeDtypeStruct((4, 32, LANES), f32),
            jax.ShapeDtypeStruct((16, hid), f32),
            jax.ShapeDtypeStruct((16, LANES), f32),
        ),
        in_specs=[any_place] * 6 + [vmem] * 2,
        out_specs=(vmem, vmem, vmem),
        scratch_shapes=[
            V((8, 48, LANES), f32),
            V((6, 48, LANES), f32),
            V((RANKS, hid, BLOCK), bf16),
            V((LANES, hid), bf16),
            V((hid, LANES), bf16),
            V((hid, LANES), bf16),
            V((LANES, LANES), f32),
            V((LANES, hid), bf16),
            V((hid, RANKS * LANES), bf16),
            V((LANES, hid), bf16),
            V((LANES, hid), f32),
            V((LANES, LANES), f32),
            V((RANKS * LANES, LANES), bf16),
            V((6, 48, LANES), f32),
            V((2, RANKS, LANES, LANES), bf16),
            V((2, RANKS * LANES, LANES), bf16),
            V((8, LANES), f32),
            V((RANKS, 8, LANES), f32),
            V((8, LANES), f32),
            V((SIDE * SIDE, 8, LANES), f32),
            V((3, 4, SIDE, SIDE, 32, LANES), bf16),
            V((3, SIDE, 2, SIDE, 32, LANES), bf16),
            V((3, SIDE, 2, SIDE, 32, LANES), bf16),
            V((3, 2, SIDE, 2, 32, LANES), bf16),
            V((3, 2, SIDE, 2, 32, LANES), bf16),
            V((3, RANKS, 16, LANES), f32),
            V((RANKS, 16, LANES), f32),
            dma((5,)),
            dma((RANKS,)),
            dma((12,)),
            dma((12,)),
            dma((RANKS,)),
            dma((RANKS,)),
            dma((RANKS,)),
            dma((RANKS,)),
            dma((SIDE * SIDE,)),
            dma((SIDE * SIDE,)),
            dma((2, RANKS)),
            dma((2, RANKS)),
            dma((3, 2, SIDE)),
            dma((3, 2, SIDE)),
            dma((3, 2, SIDE)),
            dma((3, 2, SIDE)),
            dma((3, RANKS)),
            dma((3, RANKS)),
        ],
        compiler_params=pltpu.CompilerParams(
            collective_id=0, has_side_effects=True, vmem_limit_bytes=48 * 1024 * 1024
        ),
        cost_estimate=pl.CostEstimate(
            flops=3_000_000_000, bytes_accessed=12_000_000, transcendentals=3_000_000
        ),
    )(
        field,
        wind,
        w_in,
        w_mid,
        w_out,
        targets,
        column_map.reshape(1, LANES),
        batch_count.reshape(1, 32),
    )


def solution(mesh):
    placed = (
        P("grp", "lon", None),
        P("grp", "lon", None),
        P(),
        P(),
        P(),
        P("lon", None),
        P("grp", "lon", None, None),
        P(),
    )
    return jax.shard_map(
        body,
        mesh=mesh,
        in_specs=placed,
        out_specs=(P("grp", "lon", None), P(("grp", "lon"), None), P(("grp", "lon"), None)),
        check_vma=False,
    )
```

```python
import jax
import jax.numpy as jnp
from jax import lax
from jax.experimental import pallas as pl
from jax.experimental.pallas import tpu as pltpu
from jax.sharding import PartitionSpec as P

MESH = pl.DeviceIdType.MESH
bf16, f32 = jnp.bfloat16, jnp.float32

LOSS_SCALE = 1024.0
PHYSICS_SHARE = 0.5
RANKS = 8
SIDE = 4
LANES = 128
BLOCK = 256
WIDE = 512
NT = (((1,), (1,)), ((), ()))
TN = (((0,), (0,)), ((), ()))


def sigmoid(v):
    return 0.5 + 0.5 * jnp.tanh(0.5 * v)


def wide(i, size):
    return pl.ds(pl.multiple_of(i * size, size), size)


def kernel(
    field, wind, w_in, w_mid, w_out, targets, cmap, batch,
    field_out, grad_mid, grad_out,
    ext, gust, mids, win, wint, wout, goal, first, firsts, second, slope, inputs,
    step, outgoing, mine, cnt_out, cnt_in, sum_out, sum_in,
    part, got_x, got_y, half, got_h,
    load_sem, mid_sem, halo_s, halo_r, in_s, in_r, cnt_s, cnt_r, sum_s, sum_r,
    m_s, m_r, one_s, one_r, two_s, two_r,
):
    grp, lon = lax.axis_index("grp"), lax.axis_index("lon")
    place, zh = lax.div(lon, 2), lax.rem(lon, 2)
    x, y = lax.div(place, SIDE), lax.rem(place, SIDE)
    rank = zh * 4 + grp
    is_trainer = grp == 3

    def rank_at(k):
        return lax.rem(rank + k, RANKS)

    def ring(k):
        other = rank_at(k)
        return (lax.rem(other, 4), place * 2 + lax.div(other, 4))

    def plane(k):
        return (grp, lax.rem(place + k, SIDE * SIDE) * 2 + zh)

    def along_x(k):
        return (grp, lax.rem(x + k, SIDE) * (2 * SIDE) + y * 2 + zh)

    def along_y(k):
        return (grp, x * (2 * SIDE) + lax.rem(y + k, SIDE) * 2 + zh)

    def beside(dg, dl):
        return (lax.rem(grp + dg + 4, 4), lax.rem(lon + dl + 32, 32))

    def remote(src, dst, send, recv, to):
        return pltpu.make_async_remote_copy(
            src_ref=src, dst_ref=dst, send_sem=send, recv_sem=recv,
            device_id=to, device_id_type=MESH,
        )

    loads = [
        pltpu.make_async_copy(field, ext.at[2:6, 8:40], load_sem.at[0]),
        pltpu.make_async_copy(w_in, win, load_sem.at[1]),
        pltpu.make_async_copy(wind, gust.at[1:5, 8:40], load_sem.at[2]),
        pltpu.make_async_copy(w_out, wout, load_sem.at[3]),
        pltpu.make_async_copy(targets, goal, load_sem.at[4]),
    ]

    def mid_load(c):
        return pltpu.make_async_copy(w_mid.at[:, c * WIDE : c * WIDE + WIDE], mids.at[c], mid_sem.at[c])

    for load in loads:
        load.start()
    for c in range(4):
        mid_load(c).start()

    barrier = pltpu.get_barrier_semaphore()
    greeted = [ring(k) for k in range(1, RANKS)] + [plane(k) for k in range(1, SIDE * SIDE)]
    far = 2 * zh - 1
    greeted += [beside(dg, far) for dg in (-1, 0, 1)]
    for other in greeted:
        pl.semaphore_signal(barrier, inc=1, device_id=other, device_id_type=MESH)

    names = jnp.broadcast_to(cmap[...].astype(f32), (LANES, LANES)).T
    ids = lax.broadcasted_iota(jnp.int32, (LANES, LANES), 1).astype(f32)
    match = (names == ids).astype(f32)
    own_count = jnp.sum(match, 0, keepdims=True) * jnp.where(is_trainer, 0.0, 1.0)
    cnt_out[...] = jnp.broadcast_to(own_count, (8, LANES))

    loads[0].wait()
    own_in = ext[2:6, 8:40].reshape(LANES, LANES).astype(bf16)
    inputs[wide(rank, LANES), :] = own_in
    loads[2].wait()
    pl.semaphore_wait(barrier, len(greeted))

    in_copies = [
        remote(
            inputs.at[wide(rank, LANES)], inputs.at[wide(rank, LANES)],
            in_s.at[k], in_r.at[k], ring(k),
        ) for k in range(1, RANKS)
    ]
    cnt_copies = [
        remote(cnt_out, cnt_in.at[k], cnt_s.at[k], cnt_r.at[k], ring(k)) for k in range(1, RANKS)
    ]
    halo = [
        (ext.at[2:4, 8:40], ext.at[6:8, 8:40], -1, 0),
        (ext.at[4:6, 8:40], ext.at[0:2, 8:40], 1, 0),
        (ext.at[2:6, 8:16], ext.at[2:6, 40:48], 0, -1),
        (ext.at[2:6, 32:40], ext.at[2:6, 0:8], 0, 1),
        (ext.at[2:3, 8:16], ext.at[6:7, 40:48], -1, -1),
        (ext.at[2:3, 32:40], ext.at[6:7, 0:8], -1, 1),
        (ext.at[5:6, 8:16], ext.at[1:2, 40:48], 1, -1),
        (ext.at[5:6, 32:40], ext.at[1:2, 0:8], 1, 1),
        (gust.at[1:2, 8:40], gust.at[5:6, 8:40], -1, 0),
        (gust.at[4:5, 8:40], gust.at[0:1, 8:40], 1, 0),
        (gust.at[1:5, 8:16], gust.at[1:5, 40:48], 0, -1),
        (gust.at[1:5, 32:40], gust.at[1:5, 0:8], 0, 1),
    ]
    halo_copies = [
        remote(src, dst, halo_s.at[i], halo_r.at[i], beside(dg, dl))
        for i, (src, dst, dg, dl) in enumerate(halo)
    ]
    for copy in cnt_copies + halo_copies + in_copies:
        copy.start()

    loads[1].wait()
    own_in = inputs[wide(rank, LANES), :]

    for c in range(4):
        pre = jnp.dot(own_in, win[:, c * 512 : c * 512 + 512], preferred_element_type=f32)
        first[:, c * 512 : c * 512 + 512] = (pre * sigmoid(pre)).astype(bf16)
    loads[3].wait()

    def second_step(c):
        mid_load(c).wait()
        at = slice(c * WIDE, c * WIDE + WIDE)
        pre = jnp.dot(first[...], mids[c], preferred_element_type=f32)
        sig = sigmoid(pre)
        act = (pre * sig).astype(bf16)
        second[:, at] = act
        slope[:, at] = sig * (1.0 + pre * (1.0 - sig))
        return jnp.dot(act, wout[at, :], preferred_element_type=f32)

    predicted = second_step(0) + second_step(1)

    total = cnt_out[...]
    for k in range(1, RANKS):
        cnt_copies[k - 1].wait_recv()
        total = total + cnt_in[k]
    sum_out[...] = total
    sum_copies = [
        remote(sum_out, sum_in.at[k], sum_s.at[k], sum_r.at[k], plane(k))
        for k in range(1, SIDE * SIDE)
    ]
    for copy in sum_copies:
        copy.start()

    predicted = predicted + second_step(2) + second_step(3)

    for copy in halo_copies:
        copy.wait_recv()
    low, high = grp == 0, grp == 2

    def masked(row, values):
        if row < 0:
            return jnp.where(low, 0.0, values)
        if row > 3:
            return jnp.where(high, 0.0, values)
        return values

    def advanced(c, n, s, e, w, u):
        return c - 0.25 * u * (e - w) + 0.15 * (e + w + n + s - 4.0 * c)

    for row in range(-1, 5):
        i = row + 2
        c = masked(row, ext[i, 7:41])
        e, w = masked(row, ext[i, 8:42]), masked(row, ext[i, 6:40])
        n, s = masked(row + 1, ext[i + 1, 7:41]), masked(row - 1, ext[i - 1, 7:41])
        step[row + 1, 7:41] = masked(row, advanced(c, n, s, e, w, gust[row + 1, 7:41]))
    current = []
    for row in range(4):
        c = step[row + 1, 8:40]
        e, w = step[row + 1, 9:41], step[row + 1, 7:39]
        n, s = step[row + 2, 8:40], step[row, 8:40]
        current.append(advanced(c, n, s, e, w, gust[row + 1, 8:40]))
    current = jnp.concatenate(current, 0)
    start = ext[2:6, 8:40].reshape(LANES, LANES)
    increment = (current - start).astype(bf16).astype(f32)
    loads[4].wait()
    wanted = jnp.where(is_trainer, goal[...], increment)

    for copy in in_copies:
        copy.wait_recv()

    def turn_step(c, carry):
        wint[wide(c, BLOCK), :] = win[:, wide(c, BLOCK)].T
        return carry

    lax.fori_loop(0, RANKS, turn_step, 0)

    def firsts_step(i, carry):
        c, n = lax.div(i, 2), lax.rem(i, 2)
        pre = lax.dot_general(
            wint[wide(c, BLOCK), :], inputs[wide(n, 512), :], NT, preferred_element_type=f32
        )
        firsts[wide(c, BLOCK), wide(n, 512)] = (pre * sigmoid(pre)).astype(bf16)
        return carry

    lax.fori_loop(0, RANKS, firsts_step, 0)

    total = sum_out[...]
    for k in range(1, SIDE * SIDE):
        sum_copies[k - 1].wait_recv()
        total = total + sum_in[k]
    valid = batch[...].astype(f32)
    weight = LOSS_SCALE / (32.0 * (valid + total[0:1, 0:32]))
    column_weight = jnp.sum(match[:, 0:32] * weight, 1, keepdims=True)
    own = lax.broadcasted_iota(jnp.int32, (1, 32), 1) == lon
    own_weight = jnp.sum(jnp.where(own, weight, 0.0), 1, keepdims=True)
    own_valid = jnp.sum(jnp.where(own, valid, 0.0), 1, keepdims=True)
    rows = lax.broadcasted_iota(jnp.int32, (LANES, 1), 0).astype(f32)
    replay_weight = jnp.where(rows < own_valid, own_weight, 0.0)
    row_weight = jnp.where(is_trainer, replay_weight, column_weight)

    tendency = predicted.astype(bf16).astype(f32)
    sim = current + PHYSICS_SHARE * tendency
    field_out[...] = jnp.where(is_trainer, predicted, sim).reshape(4, 32, LANES)
    out_slope = ((predicted - wanted) * row_weight).astype(bf16)

    def m_copy(k, h):
        return remote(
            outgoing.at[h, rank_at(k)], mine.at[h, wide(rank, LANES)],
            m_s.at[h, k], m_r.at[h, k], ring(k),
        )

    for k in range(1, RANKS + 1):
        t = rank_at(k)
        back = lax.dot_general(out_slope, wout[wide(t, BLOCK), :], NT, preferred_element_type=f32)
        value = (back * slope[:, wide(t, BLOCK)]).astype(bf16)
        outgoing[0, t] = value[:, :LANES]
        outgoing[1, t] = value[:, LANES:]
        if k < RANKS:
            m_copy(k, 0).start()
    for k in range(1, RANKS):
        m_copy(k, 1).start()
    for h in range(2):
        mine[h, wide(rank, LANES), :] = outgoing[h, rank]

    def x_copy(q, k):
        return remote(
            part.at[q, 0:2, lax.rem(x + k, SIDE)], got_x.at[q, k],
            one_s.at[q, 0, k], one_r.at[q, 0, k], along_x(k),
        )

    def y_copy(q, k):
        return remote(
            part.at[q, 2:4, :, lax.rem(y + k, SIDE)], got_y.at[q, k],
            one_s.at[q, 1, k], one_r.at[q, 1, k], along_y(k),
        )

    def out_copy(q, axis, k, g, z):
        if axis == 0:
            at = lax.rem(y + k, SIDE)
            lon_at = x * (2 * SIDE) + at * 2 + z
        else:
            at = lax.rem(x + k, SIDE)
            lon_at = at * (2 * SIDE) + y * 2 + z
        src, dst = half.at[q, axis, at, g, z], got_h.at[q, k * RANKS + rank]
        return remote(src, dst, two_s.at[q], two_r.at[q], (2 * axis + g, lon_at))

    def own_copy(q, axis, g, z):
        src = half.at[q, axis, y if axis == 0 else x, g, z]
        return pltpu.make_async_copy(src, got_h.at[q, rank], two_r.at[q])

    def send_out(q, axis):
        for g in range(2):
            for z in range(2):
                here = (grp == 2 * axis + g) & (zh == z)
                for k in range(1, SIDE):
                    out_copy(q, axis, k, g, z).start()

                @pl.when(here)
                def _():
                    own_copy(q, axis, g, z).start()

                @pl.when(jnp.logical_not(here))
                def _():
                    out_copy(q, axis, 0, g, z).start()

    def out_all(q):
        return remote(got_h.at[q], got_h.at[q], two_s.at[q], two_r.at[q], ring(1))

    def make_part(q, size, product):
        steps = 1024 // size

        def rows_step(c, carry):
            value = product(c).astype(bf16)
            if size == 1024:
                part[q, pl.ds(c * 2, 2)] = value.reshape(2, SIDE, SIDE, 32, LANES)
            else:
                at = pl.ds(lax.rem(c, 2) * 2, 2)
                part[q, lax.div(c, 2), at] = value.reshape(2, SIDE, 32, LANES)
            return carry

        lax.fori_loop(0, steps, rows_step, 0)
        for k in range(1, SIDE):
            x_copy(q, k).start()
        lax.fori_loop(steps, 2 * steps, rows_step, 0)
        for k in range(1, SIDE):
            y_copy(q, k).start()

    def reduce_one(q):
        for axis in range(2):
            if axis == 0:
                total, copies, got = part[q, 0:2, x], x_copy, got_x
            else:
                total, copies, got = part[q, 2:4, :, y], y_copy, got_y
            total = total.astype(f32)
            for k in range(1, SIDE):
                copies(q, k).wait_recv()
                total = total + got[q, k].astype(f32)
            total = total.astype(bf16).reshape(2, SIDE, 2, 16, LANES)
            for g in range(2):
                half[q, axis, :, g] = total[g]
            send_out(q, axis)

    make_part(
        0,
        BLOCK,
        lambda c: lax.dot_general(
            second[:, wide(c, BLOCK)], out_slope, TN, preferred_element_type=f32
        ),
    )

    lax.fori_loop(RANKS, 2 * RANKS, firsts_step, 0)
    for h in range(2):
        for k in range(1, RANKS):
            m_copy(k, h).wait_recv()
        make_part(
            1 + h,
            1024,
            lambda c: jnp.dot(firsts[wide(c, 1024), :], mine[h], preferred_element_type=f32),
        )
        if h == 0:
            reduce_one(0)
    reduce_one(1)
    reduce_one(2)

    out_all(0).wait_recv()
    grad_out[...] = jnp.sum(got_h[0].astype(f32), 0)
    for h in range(2):
        out_all(1 + h).wait_recv()
        got = got_h[1 + h].astype(f32).reshape(SIDE, RANKS, 16, LANES)
        total = jnp.sum(got, 0)
        for t in range(RANKS):
            at = t * BLOCK + h * LANES
            grad_mid[:, at : at + LANES] = total[t]

    for copy in in_copies + cnt_copies + halo_copies + sum_copies:
        copy.wait_send()
    for h in range(2):
        for k in range(1, RANKS):
            m_copy(k, h).wait_send()
    for q in range(3):
        for k in range(1, SIDE):
            x_copy(q, k).wait_send()
            y_copy(q, k).wait_send()
        sent = got_h.at[q, 1:]
        remote(sent, sent, two_s.at[q], two_r.at[q], ring(1)).wait_send()


def body(field, wind, w_in, w_mid, w_out, targets, column_map, batch_count):
    vmem = pl.BlockSpec(memory_space=pltpu.VMEM)
    any_place = pl.BlockSpec(memory_space=pl.ANY)
    hid = w_mid.shape[0]
    dma = pltpu.SemaphoreType.DMA
    V = pltpu.VMEM
    return pl.pallas_call(
        kernel,
        out_shape=(
            jax.ShapeDtypeStruct((4, 32, LANES), f32),
            jax.ShapeDtypeStruct((16, hid), f32),
            jax.ShapeDtypeStruct((16, LANES), f32),
        ),
        in_specs=[any_place] * 6 + [vmem] * 2,
        out_specs=(vmem, vmem, vmem),
        scratch_shapes=[
            V((8, 48, LANES), f32),
            V((6, 48, LANES), f32),
            V((4, hid, WIDE), bf16),
            V((LANES, hid), bf16),
            V((hid, LANES), bf16),
            V((hid, LANES), bf16),
            V((LANES, LANES), f32),
            V((LANES, hid), bf16),
            V((hid, RANKS * LANES), bf16),
            V((LANES, hid), bf16),
            V((LANES, hid), f32),
            V((RANKS * LANES, LANES), bf16),
            V((6, 48, LANES), f32),
            V((2, RANKS, LANES, LANES), bf16),
            V((2, RANKS * LANES, LANES), bf16),
            V((8, LANES), f32),
            V((RANKS, 8, LANES), f32),
            V((8, LANES), f32),
            V((SIDE * SIDE, 8, LANES), f32),
            V((3, 4, SIDE, SIDE, 32, LANES), bf16),
            V((3, SIDE, 2, SIDE, 32, LANES), bf16),
            V((3, SIDE, 2, SIDE, 32, LANES), bf16),
            V((3, 2, SIDE, 2, 2, 16, LANES), bf16),
            V((3, SIDE * RANKS, 16, LANES), bf16),
            dma((5,)),
            dma((4,)),
            dma((12,)),
            dma((12,)),
            dma((RANKS,)),
            dma((RANKS,)),
            dma((RANKS,)),
            dma((RANKS,)),
            dma((SIDE * SIDE,)),
            dma((SIDE * SIDE,)),
            dma((2, RANKS)),
            dma((2, RANKS)),
            dma((3, 2, SIDE)),
            dma((3, 2, SIDE)),
            dma((3,)),
            dma((3,)),
        ],
        compiler_params=pltpu.CompilerParams(
            collective_id=0, has_side_effects=True, vmem_limit_bytes=64 * 1024 * 1024
        ),
        cost_estimate=pl.CostEstimate(
            flops=3_000_000_000, bytes_accessed=12_000_000, transcendentals=3_000_000
        ),
    )(
        field,
        wind,
        w_in,
        w_mid,
        w_out,
        targets,
        column_map.reshape(1, LANES),
        batch_count.reshape(1, 32),
    )


def solution(mesh):
    placed = (
        P("grp", "lon", None),
        P("grp", "lon", None),
        P(),
        P(),
        P(),
        P("lon", None),
        P("grp", "lon", None, None),
        P(),
    )
    return jax.shard_map(
        body,
        mesh=mesh,
        in_specs=placed,
        out_specs=(P("grp", "lon", None), P(("grp", "lon"), None), P(("grp", "lon"), None)),
        check_vma=False,
    )
```

```python
import jax
import jax.numpy as jnp
from jax import lax
from jax.experimental import pallas as pl
from jax.experimental.pallas import tpu as pltpu
from jax.sharding import PartitionSpec as P

MESH = pl.DeviceIdType.MESH
bf16, f32 = jnp.bfloat16, jnp.float32

LOSS_SCALE = 1024.0
PHYSICS_SHARE = 0.5
RANKS = 8
SIDE = 4
LANES = 128
VMEM_BYTES = 62 * 1024 * 1024
BLOCK = 256
WIDE = 512
NT = (((1,), (1,)), ((), ()))
TN = (((0,), (0,)), ((), ()))


def sigmoid(v):
    return 0.5 + 0.5 * jnp.tanh(0.5 * v)


def wide(i, size):
    return pl.ds(pl.multiple_of(i * size, size), size)


def kernel(
    field, wind, w_in, w_mid, w_out, targets, cmap_in, batch_in,
    field_out, grad_mid, grad_out,
    cmap, batch, ext, gust, mids, win, wint, wout, goal, first, firsts, second, slope, inputs,
    step, outgoing, mine, cnt_out, cnt_in, sum_out, sum_in,
    part, got_one, half, got_h,
    load_sem, mid_sem, halo_s, halo_r, in_s, in_r, cnt_s, cnt_r, sum_s, sum_r,
    m_s, m_r, one_s, one_r, two_s, two_r,
):
    grp, lon = lax.axis_index("grp"), lax.axis_index("lon")
    place, zh = lax.div(lon, 2), lax.rem(lon, 2)
    x, y = lax.div(place, SIDE), lax.rem(place, SIDE)
    rank = zh * 4 + grp
    is_trainer = grp == 3

    def rank_at(k):
        return lax.rem(rank + k, RANKS)

    def ring(k):
        other = rank_at(k)
        return (lax.rem(other, 4), place * 2 + lax.div(other, 4))

    def plane(k):
        return (grp, lax.rem(place + k, SIDE * SIDE) * 2 + zh)

    def along_x(k):
        return (grp, lax.rem(x + k, SIDE) * (2 * SIDE) + y * 2 + zh)

    def along_y(k):
        return (grp, x * (2 * SIDE) + lax.rem(y + k, SIDE) * 2 + zh)

    def beside(dg, dl):
        return (lax.rem(grp + dg + 4, 4), lax.rem(lon + dl + 32, 32))

    def remote(src, dst, send, recv, to):
        return pltpu.make_async_remote_copy(
            src_ref=src, dst_ref=dst, send_sem=send, recv_sem=recv,
            device_id=to, device_id_type=MESH,
        )

    loads = [
        pltpu.make_async_copy(field, ext.at[2:6, 8:40], load_sem.at[0]),
        pltpu.make_async_copy(w_in, win, load_sem.at[1]),
        pltpu.make_async_copy(wind, gust.at[1:5, 8:40], load_sem.at[2]),
        pltpu.make_async_copy(w_out, wout, load_sem.at[3]),
        pltpu.make_async_copy(targets, goal, load_sem.at[4]),
        pltpu.make_async_copy(cmap_in, cmap, load_sem.at[5]),
        pltpu.make_async_copy(batch_in, batch, load_sem.at[6]),
    ]

    def mid_load(c):
        return pltpu.make_async_copy(w_mid.at[:, c * WIDE : c * WIDE + WIDE], mids.at[c], mid_sem.at[c])

    barrier = pltpu.get_barrier_semaphore()
    far = 2 * zh - 1
    greeted = [beside(dg, far) for dg in (-1, 0, 1)]
    greeted += [plane(k) for k in range(1, SIDE * SIDE)] + [ring(k) for k in range(1, RANKS)]
    for other in greeted:
        pl.semaphore_signal(barrier, inc=1, device_id=other, device_id_type=MESH)

    for i in (0, 2, 5, 1):
        loads[i].start()
    for c in range(4):
        mid_load(c).start()
    for i in (3, 4, 6):
        loads[i].start()

    loads[5].wait()
    names = jnp.broadcast_to(cmap[...].astype(f32), (LANES, LANES)).T
    ids = lax.broadcasted_iota(jnp.int32, (LANES, LANES), 1).astype(f32)
    match = (names == ids).astype(f32)
    own_count = jnp.sum(match, 0, keepdims=True) * jnp.where(is_trainer, 0.0, 1.0)
    cnt_out[...] = jnp.broadcast_to(own_count, (8, LANES))

    loads[0].wait()
    own_in = ext[2:6, 8:40].reshape(LANES, LANES).astype(bf16)
    inputs[wide(rank, LANES), :] = own_in
    loads[2].wait()
    pl.semaphore_wait(barrier, len(greeted))

    in_copies = [
        remote(
            inputs.at[wide(rank, LANES)], inputs.at[wide(rank, LANES)],
            in_s.at[k], in_r.at[k], ring(k),
        ) for k in range(1, RANKS)
    ]
    cnt_copies = [
        remote(cnt_out, cnt_in.at[k], cnt_s.at[k], cnt_r.at[k], ring(k)) for k in range(1, RANKS)
    ]
    halo = [
        (ext.at[2:4, 8:40], ext.at[6:8, 8:40], -1, 0),
        (ext.at[4:6, 8:40], ext.at[0:2, 8:40], 1, 0),
        (ext.at[2:6, 8:16], ext.at[2:6, 40:48], 0, -1),
        (ext.at[2:6, 32:40], ext.at[2:6, 0:8], 0, 1),
        (ext.at[2:3, 8:16], ext.at[6:7, 40:48], -1, -1),
        (ext.at[2:3, 32:40], ext.at[6:7, 0:8], -1, 1),
        (ext.at[5:6, 8:16], ext.at[1:2, 40:48], 1, -1),
        (ext.at[5:6, 32:40], ext.at[1:2, 0:8], 1, 1),
        (gust.at[1:2, 8:40], gust.at[5:6, 8:40], -1, 0),
        (gust.at[4:5, 8:40], gust.at[0:1, 8:40], 1, 0),
        (gust.at[1:5, 8:16], gust.at[1:5, 40:48], 0, -1),
        (gust.at[1:5, 32:40], gust.at[1:5, 0:8], 0, 1),
    ]
    halo_copies = [
        remote(src, dst, halo_s.at[i], halo_r.at[i], beside(dg, dl))
        for i, (src, dst, dg, dl) in enumerate(halo)
    ]
    for copy in halo_copies + cnt_copies + in_copies:
        copy.start()

    loads[1].wait()
    own_in = inputs[wide(rank, LANES), :]

    for c in range(4):
        pre = jnp.dot(own_in, win[:, c * 512 : c * 512 + 512], preferred_element_type=f32)
        first[:, c * 512 : c * 512 + 512] = (pre * sigmoid(pre)).astype(bf16)
    loads[3].wait()

    def second_step(c):
        mid_load(c).wait()
        at = slice(c * WIDE, c * WIDE + WIDE)
        pre = jnp.dot(first[...], mids[c], preferred_element_type=f32)
        sig = sigmoid(pre)
        act = (pre * sig).astype(bf16)
        second[:, at] = act
        slope[:, at] = sig * (1.0 + pre * (1.0 - sig))
        return jnp.dot(act, wout[at, :], preferred_element_type=f32)

    predicted = second_step(0) + second_step(1)

    total = cnt_out[...]
    for k in range(1, RANKS):
        cnt_copies[k - 1].wait_recv()
        total = total + cnt_in[k]
    sum_out[...] = total
    sum_copies = [
        remote(sum_out, sum_in.at[k], sum_s.at[k], sum_r.at[k], plane(k))
        for k in range(1, SIDE * SIDE)
    ]
    for copy in sum_copies:
        copy.start()

    predicted = predicted + second_step(2) + second_step(3)

    def turn_step(c, carry):
        wint[wide(c, BLOCK), :] = win[:, wide(c, BLOCK)].T
        return carry

    lax.fori_loop(0, RANKS, turn_step, 0)

    for copy in halo_copies:
        copy.wait_recv()
    low, high = grp == 0, grp == 2

    def masked(row, values):
        if row < 0:
            return jnp.where(low, 0.0, values)
        if row > 3:
            return jnp.where(high, 0.0, values)
        return values

    def advanced(c, n, s, e, w, u):
        return c - 0.25 * u * (e - w) + 0.15 * (e + w + n + s - 4.0 * c)

    for row in range(-1, 5):
        i = row + 2
        c = masked(row, ext[i, 7:41])
        e, w = masked(row, ext[i, 8:42]), masked(row, ext[i, 6:40])
        n, s = masked(row + 1, ext[i + 1, 7:41]), masked(row - 1, ext[i - 1, 7:41])
        step[row + 1, 7:41] = masked(row, advanced(c, n, s, e, w, gust[row + 1, 7:41]))
    current = []
    for row in range(4):
        c = step[row + 1, 8:40]
        e, w = step[row + 1, 9:41], step[row + 1, 7:39]
        n, s = step[row + 2, 8:40], step[row, 8:40]
        current.append(advanced(c, n, s, e, w, gust[row + 1, 8:40]))
    current = jnp.concatenate(current, 0)
    start = ext[2:6, 8:40].reshape(LANES, LANES)
    increment = (current - start).astype(bf16).astype(f32)
    loads[4].wait()
    wanted = jnp.where(is_trainer, goal[...], increment)

    total = sum_out[...]
    for k in range(1, SIDE * SIDE):
        sum_copies[k - 1].wait_recv()
        total = total + sum_in[k]
    loads[6].wait()
    valid = batch[...].astype(f32)
    weight = LOSS_SCALE / (32.0 * (valid + total[0:1, 0:32]))
    column_weight = jnp.sum(match[:, 0:32] * weight, 1, keepdims=True)
    own = lax.broadcasted_iota(jnp.int32, (1, 32), 1) == lon
    own_weight = jnp.sum(jnp.where(own, weight, 0.0), 1, keepdims=True)
    own_valid = jnp.sum(jnp.where(own, valid, 0.0), 1, keepdims=True)
    rows = lax.broadcasted_iota(jnp.int32, (LANES, 1), 0).astype(f32)
    replay_weight = jnp.where(rows < own_valid, own_weight, 0.0)
    row_weight = jnp.where(is_trainer, replay_weight, column_weight)

    tendency = predicted.astype(bf16).astype(f32)
    sim = current + PHYSICS_SHARE * tendency
    field_out[...] = jnp.where(is_trainer, predicted, sim).reshape(4, 32, LANES)
    out_slope = ((predicted - wanted) * row_weight).astype(bf16)

    def m_copy(k, h):
        return remote(
            outgoing.at[h, rank_at(k)], mine.at[h, wide(rank, LANES)],
            m_s.at[h, k], m_r.at[h, k], ring(k),
        )

    for group in ((4, 3, 5, 2), (6, 1, 7, 0)):
        for k in group:
            t = rank_at(k)
            back = lax.dot_general(
                out_slope, wout[wide(t, BLOCK), :], NT, preferred_element_type=f32
            )
            value = (back * slope[:, wide(t, BLOCK)]).astype(bf16)
            outgoing[0, t] = value[:, :LANES]
            outgoing[1, t] = value[:, LANES:]
        for k in group:
            if k:
                m_copy(k, 0).start()
    for k in (4, 3, 5, 2, 6, 1, 7):
        m_copy(k, 1).start()
    for h in range(2):
        mine[h, wide(rank, LANES), :] = outgoing[h, rank]

    def one_copy(q, k, g):
        if g < 2:
            src, to = part.at[q, g, lax.rem(x + k, SIDE)], along_x(k)
        else:
            src, to = part.at[q, g, :, lax.rem(y + k, SIDE)], along_y(k)
        axis = g // 2
        return remote(
            src, got_one.at[q, axis, k, g % 2], one_s.at[q, axis, k], one_r.at[q, axis, k], to
        )

    def one_pair(q, axis, k):
        both = got_one.at[q, axis, k]
        return remote(both, both, one_s.at[q, axis, k], one_r.at[q, axis, k], along_x(k))

    def out_copy(q, axis, k, g, z):
        if axis == 0:
            at = lax.rem(y + k, SIDE)
            lon_at = x * (2 * SIDE) + at * 2 + z
        else:
            at = lax.rem(x + k, SIDE)
            lon_at = at * (2 * SIDE) + y * 2 + z
        src, dst = half.at[q, axis, at, g, z], got_h.at[q, k * RANKS + rank]
        return remote(src, dst, two_s.at[q], two_r.at[q], (2 * axis + g, lon_at))

    def own_copy(q, axis, g, z):
        src = half.at[q, axis, y if axis == 0 else x, g, z]
        return pltpu.make_async_copy(src, got_h.at[q, rank], two_r.at[q])

    def send_out(q, axis):
        rows = [(g, z) for g in range(2) for z in range(2)]
        for k in (2, 1, 3):
            for g, z in rows:
                out_copy(q, axis, k, g, z).start()
        for g, z in rows:
            here = (grp == 2 * axis + g) & (zh == z)

            @pl.when(here)
            def _():
                own_copy(q, axis, g, z).start()

            @pl.when(jnp.logical_not(here))
            def _():
                out_copy(q, axis, 0, g, z).start()

    def out_all(q):
        return remote(got_h.at[q], got_h.at[q], two_s.at[q], two_r.at[q], ring(1))

    def make_part(q, product):
        for g in (0, 2, 1, 3):
            part[q, g] = product(g).astype(bf16).reshape(SIDE, SIDE, 32, LANES)
            for k in (2, 1, 3):
                one_copy(q, k, g).start()

    def reduce_one(q):
        for axis in range(2):
            total = part[q, 0:2, x] if axis == 0 else part[q, 2:4, :, y]
            total = total.astype(f32)
            for k in range(1, SIDE):
                one_pair(q, axis, k).wait_recv()
                total = total + got_one[q, axis, k].astype(f32)
            total = total.astype(bf16).reshape(2, SIDE, 2, 16, LANES)
            for g in range(2):
                half[q, axis, :, g] = total[g]
            send_out(q, axis)

    make_part(
        0,
        lambda g: lax.dot_general(
            second[:, g * 512 : g * 512 + 512], out_slope, TN, preferred_element_type=f32
        ),
    )

    for copy in in_copies:
        copy.wait_recv()

    def firsts_step(i, carry):
        c, n = lax.div(i, 2), lax.rem(i, 2)
        pre = lax.dot_general(
            wint[wide(c, BLOCK), :], inputs[wide(n, 512), :], NT, preferred_element_type=f32
        )
        firsts[wide(c, BLOCK), wide(n, 512)] = (pre * sigmoid(pre)).astype(bf16)
        return carry

    lax.fori_loop(0, 2 * RANKS, firsts_step, 0)

    for h in range(2):
        for k in range(1, RANKS):
            m_copy(k, h).wait_recv()
        make_part(
            1 + h,
            lambda g: jnp.dot(
                firsts[g * 512 : g * 512 + 512, :], mine[h], preferred_element_type=f32
            ),
        )
    for q in range(3):
        reduce_one(q)

    out_all(0).wait_recv()
    grad_out[...] = jnp.sum(got_h[0].astype(f32), 0)
    for h in range(2):
        out_all(1 + h).wait_recv()
        got = got_h[1 + h].astype(f32).reshape(SIDE, RANKS, 16, LANES)
        total = jnp.sum(got, 0)
        for t in range(RANKS):
            at = t * BLOCK + h * LANES
            grad_mid[:, at : at + LANES] = total[t]

    for copy in in_copies + cnt_copies + halo_copies + sum_copies:
        copy.wait_send()
    for h in range(2):
        for k in range(1, RANKS):
            m_copy(k, h).wait_send()
    for q in range(3):
        for k in range(1, SIDE):
            for axis in range(2):
                one_pair(q, axis, k).wait_send()
        sent = got_h.at[q, 1:]
        remote(sent, sent, two_s.at[q], two_r.at[q], ring(1)).wait_send()


def hand_on(a, b, c, a_out, b_out, c_out):
    a_out[...], b_out[...], c_out[...] = a[...], b[...], c[...]


def body(field, wind, w_in, w_mid, w_out, targets, column_map, batch_count):
    vmem = pl.BlockSpec(memory_space=pltpu.VMEM)
    hbm = pl.BlockSpec(memory_space=pltpu.HBM)
    hid = w_mid.shape[0]
    dma = pltpu.SemaphoreType.DMA
    V = pltpu.VMEM
    results = pl.pallas_call(
        kernel,
        out_shape=(
            jax.ShapeDtypeStruct((4, 32, LANES), f32),
            jax.ShapeDtypeStruct((16, hid), f32),
            jax.ShapeDtypeStruct((16, LANES), f32),
        ),
        in_specs=[hbm] * 8,
        out_specs=(vmem, vmem, vmem),
        scratch_shapes=[
            V((1, LANES), jnp.int32),
            V((1, 32), jnp.int32),
            V((8, 48, LANES), f32),
            V((6, 48, LANES), f32),
            V((4, hid, WIDE), bf16),
            V((LANES, hid), bf16),
            V((hid, LANES), bf16),
            V((hid, LANES), bf16),
            V((LANES, LANES), f32),
            V((LANES, hid), bf16),
            V((hid, RANKS * LANES), bf16),
            V((LANES, hid), bf16),
            V((LANES, hid), f32),
            V((RANKS * LANES, LANES), bf16),
            V((6, 48, LANES), f32),
            V((2, RANKS, LANES, LANES), bf16),
            V((2, RANKS * LANES, LANES), bf16),
            V((8, LANES), f32),
            V((RANKS, 8, LANES), f32),
            V((8, LANES), f32),
            V((SIDE * SIDE, 8, LANES), f32),
            V((3, 4, SIDE, SIDE, 32, LANES), bf16),
            V((3, 2, SIDE, 2, SIDE, 32, LANES), bf16),
            V((3, 2, SIDE, 2, 2, 16, LANES), bf16),
            V((3, SIDE * RANKS, 16, LANES), bf16),
            dma((7,)),
            dma((4,)),
            dma((12,)),
            dma((12,)),
            dma((RANKS,)),
            dma((RANKS,)),
            dma((RANKS,)),
            dma((RANKS,)),
            dma((SIDE * SIDE,)),
            dma((SIDE * SIDE,)),
            dma((2, RANKS)),
            dma((2, RANKS)),
            dma((3, 2, SIDE)),
            dma((3, 2, SIDE)),
            dma((3,)),
            dma((3,)),
        ],
        compiler_params=pltpu.CompilerParams(
            collective_id=0, has_side_effects=True, vmem_limit_bytes=VMEM_BYTES
        ),
        cost_estimate=pl.CostEstimate(
            flops=3_000_000_000, bytes_accessed=12_000_000, transcendentals=3_000_000
        ),
    )(
        field,
        wind,
        w_in,
        w_mid,
        w_out,
        targets,
        column_map.reshape(1, LANES),
        batch_count.reshape(1, 32),
    )
    return pl.pallas_call(
        hand_on,
        out_shape=tuple(jax.ShapeDtypeStruct(r.shape, r.dtype) for r in results),
        in_specs=[vmem] * 3,
        out_specs=(vmem,) * 3,
        compiler_params=pltpu.CompilerParams(vmem_limit_bytes=VMEM_BYTES),
    )(*results)


def solution(mesh):
    placed = (
        P("grp", "lon", None),
        P("grp", "lon", None),
        P(),
        P(),
        P(),
        P("lon", None),
        P("grp", "lon", None, None),
        P(),
    )
    return jax.shard_map(
        body,
        mesh=mesh,
        in_specs=placed,
        out_specs=(P("grp", "lon", None), P(("grp", "lon"), None), P(("grp", "lon"), None)),
        check_vma=False,
    )
```

```python
import jax
import jax.numpy as jnp
from jax import lax
from jax.experimental import pallas as pl
from jax.experimental.pallas import tpu as pltpu
from jax.sharding import PartitionSpec as P

MESH = pl.DeviceIdType.MESH
bf16, f32 = jnp.bfloat16, jnp.float32

LOSS_SCALE = 1024.0
PHYSICS_SHARE = 0.5
RANKS = 8
SIDE = 4
LANES = 128
VMEM_BYTES = 62 * 1024 * 1024
BLOCK = 256
WIDE = 512
NT = (((1,), (1,)), ((), ()))
TN = (((0,), (0,)), ((), ()))


def sigmoid(v):
    return 0.5 + 0.5 * jnp.tanh(0.5 * v)


def wide(i, size):
    return pl.ds(pl.multiple_of(i * size, size), size)


def kernel(
    field, wind, w_in, w_mid, w_out, targets, cmap_in, batch_in,
    field_out, grad_mid, grad_out,
    cmap, batch, ext, gust, mids, win, wint, wout, goal, first, firsts, second, slope, inputs,
    step, outgoing, mine, cnt_out, cnt_in, sum_out, sum_in,
    part, got_one, half_0, half_1, got_0, got_1,
    load_sem, mid_sem, halo_s, halo_r, in_s, in_r, cnt_s, cnt_r, sum_s, sum_r,
    m_s, m_r, one_s, one_r, two_s, two_r, passed,
):
    grp, lon = lax.axis_index("grp"), lax.axis_index("lon")
    place, zh = lax.div(lon, 2), lax.rem(lon, 2)
    x, y = lax.div(place, SIDE), lax.rem(place, SIDE)
    rank = zh * 4 + grp
    is_trainer = grp == 3

    def rank_at(k):
        return lax.rem(rank + k, RANKS)

    def ring(k):
        other = rank_at(k)
        return (lax.rem(other, 4), place * 2 + lax.div(other, 4))

    def plane(k):
        return (grp, lax.rem(place + k, SIDE * SIDE) * 2 + zh)

    def along_x(k):
        return (grp, lax.rem(x + k, SIDE) * (2 * SIDE) + y * 2 + zh)

    def along_y(k):
        return (grp, x * (2 * SIDE) + lax.rem(y + k, SIDE) * 2 + zh)

    def beside(dg, dl):
        return (lax.rem(grp + dg + 4, 4), lax.rem(lon + dl + 32, 32))

    def remote(src, dst, send, recv, to):
        return pltpu.make_async_remote_copy(
            src_ref=src, dst_ref=dst, send_sem=send, recv_sem=recv,
            device_id=to, device_id_type=MESH,
        )

    loads = [
        pltpu.make_async_copy(field, ext.at[2:6, 8:40], load_sem.at[0]),
        pltpu.make_async_copy(w_in, win, load_sem.at[1]),
        pltpu.make_async_copy(wind, gust.at[1:5, 8:40], load_sem.at[2]),
        pltpu.make_async_copy(w_out, wout, load_sem.at[3]),
        pltpu.make_async_copy(targets, goal, load_sem.at[4]),
        pltpu.make_async_copy(cmap_in, cmap, load_sem.at[5]),
        pltpu.make_async_copy(batch_in, batch, load_sem.at[6]),
    ]

    def mid_load(c):
        return pltpu.make_async_copy(w_mid.at[:, c * WIDE : c * WIDE + WIDE], mids.at[c], mid_sem.at[c])

    barrier = pltpu.get_barrier_semaphore()
    x_peers, y_peers = [along_x(k) for k in range(1, SIDE)], [along_y(k) for k in range(1, SIDE)]
    greeted = [ring(k) for k in range(1, RANKS)] + x_peers + y_peers
    for other in greeted:
        pl.semaphore_signal(barrier, inc=1, device_id=other, device_id_type=MESH)

    for i in (0, 2, 5, 1):
        loads[i].start()
    for c in range(4):
        mid_load(c).start()
    for i in (3, 4, 6):
        loads[i].start()

    loads[5].wait()
    names = jnp.broadcast_to(cmap[...].astype(f32), (LANES, LANES)).T
    ids = lax.broadcasted_iota(jnp.int32, (LANES, LANES), 1).astype(f32)
    match = (names == ids).astype(f32)
    own_count = jnp.sum(match, 0, keepdims=True) * jnp.where(is_trainer, 0.0, 1.0)
    cnt_out[...] = jnp.broadcast_to(own_count, (8, LANES))

    loads[0].wait()
    own_in = ext[2:6, 8:40].reshape(LANES, LANES).astype(bf16)
    inputs[wide(rank, LANES), :] = own_in
    loads[2].wait()
    pl.semaphore_wait(barrier, len(greeted))

    in_copies = [
        remote(
            inputs.at[wide(rank, LANES)], inputs.at[wide(rank, LANES)],
            in_s.at[k], in_r.at[k], ring(k),
        ) for k in range(1, RANKS)
    ]
    cnt_copies = [
        remote(cnt_out, cnt_in.at[k], cnt_s.at[k], cnt_r.at[k], ring(k)) for k in range(1, RANKS)
    ]
    halo = [
        (ext.at[2:4, 8:40], ext.at[6:8, 8:40], -1, 0),
        (ext.at[4:6, 8:40], ext.at[0:2, 8:40], 1, 0),
        (ext.at[2:6, 8:16], ext.at[2:6, 40:48], 0, -1),
        (ext.at[2:6, 32:40], ext.at[2:6, 0:8], 0, 1),
        (ext.at[2:3, 8:16], ext.at[6:7, 40:48], -1, -1),
        (ext.at[2:3, 32:40], ext.at[6:7, 0:8], -1, 1),
        (ext.at[5:6, 8:16], ext.at[1:2, 40:48], 1, -1),
        (ext.at[5:6, 32:40], ext.at[1:2, 0:8], 1, 1),
        (gust.at[1:2, 8:40], gust.at[5:6, 8:40], -1, 0),
        (gust.at[4:5, 8:40], gust.at[0:1, 8:40], 1, 0),
        (gust.at[1:5, 8:16], gust.at[1:5, 40:48], 0, -1),
        (gust.at[1:5, 32:40], gust.at[1:5, 0:8], 0, 1),
    ]
    halo_copies = [
        remote(src, dst, halo_s.at[i], halo_r.at[i], beside(dg, dl))
        for i, (src, dst, dg, dl) in enumerate(halo)
    ]
    for copy in cnt_copies:
        copy.start()
    for other in x_peers + y_peers:
        pl.semaphore_signal(passed.at[0], inc=1, device_id=other, device_id_type=MESH)
    for copy in in_copies:
        copy.start()

    loads[1].wait()
    own_in = inputs[wide(rank, LANES), :]

    for c in range(4):
        pre = jnp.dot(own_in, win[:, c * 512 : c * 512 + 512], preferred_element_type=f32)
        first[:, c * 512 : c * 512 + 512] = (pre * sigmoid(pre)).astype(bf16)
    loads[3].wait()

    def second_step(c):
        mid_load(c).wait()
        at = slice(c * WIDE, c * WIDE + WIDE)
        pre = jnp.dot(first[...], mids[c], preferred_element_type=f32)
        sig = sigmoid(pre)
        act = (pre * sig).astype(bf16)
        second[:, at] = act
        slope[:, at] = sig * (1.0 + pre * (1.0 - sig))
        return jnp.dot(act, wout[at, :], preferred_element_type=f32)

    pl.semaphore_wait(passed.at[0], len(x_peers) + len(y_peers))
    for other in x_peers:
        pl.semaphore_signal(passed.at[1], inc=1, device_id=other, device_id_type=MESH)
    predicted = second_step(0)
    pl.semaphore_wait(passed.at[1], len(x_peers))
    for copy in halo_copies:
        copy.start()
    predicted = predicted + second_step(1)

    total = cnt_out[...]
    for k in range(1, RANKS):
        cnt_copies[k - 1].wait_recv()
        total = total + cnt_in[k]
    sum_out[...] = total
    sum_copies = [
        remote(sum_out, sum_in.at[k], sum_s.at[k], sum_r.at[k], plane(k))
        for k in range(1, SIDE * SIDE)
    ]
    for copy in sum_copies:
        copy.start()

    predicted = predicted + second_step(2) + second_step(3)

    def turn_step(c, carry):
        wint[wide(c, BLOCK), :] = win[:, wide(c, BLOCK)].T
        return carry

    lax.fori_loop(0, RANKS, turn_step, 0)

    for copy in halo_copies:
        copy.wait_recv()
    low, high = grp == 0, grp == 2

    def masked(row, values):
        if row < 0:
            return jnp.where(low, 0.0, values)
        if row > 3:
            return jnp.where(high, 0.0, values)
        return values

    def advanced(c, n, s, e, w, u):
        return c - 0.25 * u * (e - w) + 0.15 * (e + w + n + s - 4.0 * c)

    for row in range(-1, 5):
        i = row + 2
        c = masked(row, ext[i, 7:41])
        e, w = masked(row, ext[i, 8:42]), masked(row, ext[i, 6:40])
        n, s = masked(row + 1, ext[i + 1, 7:41]), masked(row - 1, ext[i - 1, 7:41])
        step[row + 1, 7:41] = masked(row, advanced(c, n, s, e, w, gust[row + 1, 7:41]))
    current = []
    for row in range(4):
        c = step[row + 1, 8:40]
        e, w = step[row + 1, 9:41], step[row + 1, 7:39]
        n, s = step[row + 2, 8:40], step[row, 8:40]
        current.append(advanced(c, n, s, e, w, gust[row + 1, 8:40]))
    current = jnp.concatenate(current, 0)
    start = ext[2:6, 8:40].reshape(LANES, LANES)
    increment = (current - start).astype(bf16).astype(f32)
    loads[4].wait()
    wanted = jnp.where(is_trainer, goal[...], increment)

    total = sum_out[...]
    for k in range(1, SIDE * SIDE):
        sum_copies[k - 1].wait_recv()
        total = total + sum_in[k]
    loads[6].wait()
    valid = batch[...].astype(f32)
    weight = LOSS_SCALE / (32.0 * (valid + total[0:1, 0:32]))
    column_weight = jnp.sum(match[:, 0:32] * weight, 1, keepdims=True)
    own = lax.broadcasted_iota(jnp.int32, (1, 32), 1) == lon
    own_weight = jnp.sum(jnp.where(own, weight, 0.0), 1, keepdims=True)
    own_valid = jnp.sum(jnp.where(own, valid, 0.0), 1, keepdims=True)
    rows = lax.broadcasted_iota(jnp.int32, (LANES, 1), 0).astype(f32)
    replay_weight = jnp.where(rows < own_valid, own_weight, 0.0)
    row_weight = jnp.where(is_trainer, replay_weight, column_weight)

    tendency = predicted.astype(bf16).astype(f32)
    sim = current + PHYSICS_SHARE * tendency
    field_out[...] = jnp.where(is_trainer, predicted, sim).reshape(4, 32, LANES)
    out_slope = ((predicted - wanted) * row_weight).astype(bf16)

    def m_copy(k, h):
        return remote(
            outgoing.at[h, rank_at(k)], mine.at[h, wide(rank, LANES)],
            m_s.at[h, k], m_r.at[h, k], ring(k),
        )

    for group in ((4, 3, 5, 2), (6, 1, 7, 0)):
        for k in group:
            t = rank_at(k)
            back = lax.dot_general(
                out_slope, wout[wide(t, BLOCK), :], NT, preferred_element_type=f32
            )
            value = (back * slope[:, wide(t, BLOCK)]).astype(bf16)
            outgoing[0, t] = value[:, :LANES]
            outgoing[1, t] = value[:, LANES:]
        for k in group:
            if k:
                m_copy(k, 0).start()
    for k in (4, 3, 5, 2, 6, 1, 7):
        m_copy(k, 1).start()
    for h in range(2):
        mine[h, wide(rank, LANES), :] = outgoing[h, rank]

    def one_copy(q, k, g):
        if g < 2:
            src, to = part.at[q, g, lax.rem(x + k, SIDE)], along_x(k)
        else:
            src, to = part.at[q, g, :, lax.rem(y + k, SIDE)], along_y(k)
        axis = g // 2
        return remote(
            src, got_one.at[q, axis, k, g % 2], one_s.at[q, axis, k], one_r.at[q, axis, k], to
        )

    def one_pair(q, axis, k):
        both = got_one.at[q, axis, k]
        return remote(both, both, one_s.at[q, axis, k], one_r.at[q, axis, k], along_x(k))

    halves, gots = (half_0, half_1), (got_0, got_1)

    def out_copy(n, axis, k, g, z):
        if axis == 0:
            at = lax.rem(y + k, SIDE)
            lon_at = x * (2 * SIDE) + at * 2 + z
        else:
            at = lax.rem(x + k, SIDE)
            lon_at = at * (2 * SIDE) + y * 2 + z
        src, dst = halves[n].at[axis, at, g, z], gots[n].at[k * RANKS + rank]
        return remote(src, dst, two_s.at[n], two_r.at[n], (2 * axis + g, lon_at))

    def own_copy(n, axis, g, z):
        src = halves[n].at[axis, y if axis == 0 else x, g, z]
        return pltpu.make_async_copy(src, gots[n].at[rank], two_r.at[n])

    def send_out(n, axis):
        rows = [(g, z) for g in range(2) for z in range(2)]
        for k in (2, 1, 3):
            for g, z in rows:
                out_copy(n, axis, k, g, z).start()
        for g, z in rows:
            here = (grp == 2 * axis + g) & (zh == z)

            @pl.when(here)
            def _():
                own_copy(n, axis, g, z).start()

            @pl.when(jnp.logical_not(here))
            def _():
                out_copy(n, axis, 0, g, z).start()

    def out_all(n):
        return remote(gots[n], gots[n], two_s.at[n], two_r.at[n], ring(1))

    def make_part(q, product):
        for g in (0, 2, 1, 3):
            part[q, g] = product(g).astype(bf16).reshape(SIDE, SIDE, 32, LANES)
            for k in (2, 1, 3):
                one_copy(q, k, g).start()

    def reduce_one(n, parts):
        for axis in range(2):
            for i, q in enumerate(parts):
                total = part[q, 0:2, x] if axis == 0 else part[q, 2:4, :, y]
                total = total.astype(f32)
                for k in range(1, SIDE):
                    one_pair(q, axis, k).wait_recv()
                    total = total + got_one[q, axis, k].astype(f32)
                total = total.astype(bf16).reshape(2, SIDE, 2, 16, LANES)
                for g in range(2):
                    halves[n][axis, :, g, :, i] = total[g]
            send_out(n, axis)

    make_part(
        0,
        lambda g: lax.dot_general(
            second[:, g * 512 : g * 512 + 512], out_slope, TN, preferred_element_type=f32
        ),
    )

    for copy in in_copies:
        copy.wait_recv()

    def firsts_step(i, carry):
        c, n = lax.div(i, 2), lax.rem(i, 2)
        pre = lax.dot_general(
            wint[wide(c, BLOCK), :], inputs[wide(n, 512), :], NT, preferred_element_type=f32
        )
        firsts[wide(c, BLOCK), wide(n, 512)] = (pre * sigmoid(pre)).astype(bf16)
        return carry

    lax.fori_loop(0, 2 * RANKS, firsts_step, 0)

    for h in range(2):
        for k in range(1, RANKS):
            m_copy(k, h).wait_recv()
        make_part(
            1 + h,
            lambda g: jnp.dot(
                firsts[g * 512 : g * 512 + 512, :], mine[h], preferred_element_type=f32
            ),
        )
    reduce_one(0, (0,))
    reduce_one(1, (1, 2))

    out_all(0).wait_recv()
    grad_out[...] = jnp.sum(got_0[:, 0].astype(f32), 0)
    out_all(1).wait_recv()
    for h in range(2):
        total = jnp.sum(got_1[:, h].astype(f32).reshape(SIDE, RANKS, 16, LANES), 0)
        for t in range(RANKS):
            at = t * BLOCK + h * LANES
            grad_mid[:, at : at + LANES] = total[t]

    for copy in in_copies + cnt_copies + halo_copies + sum_copies:
        copy.wait_send()
    for h in range(2):
        for k in range(1, RANKS):
            m_copy(k, h).wait_send()
    for q in range(3):
        for k in range(1, SIDE):
            for axis in range(2):
                one_pair(q, axis, k).wait_send()
    for n in range(2):
        sent = gots[n].at[1:]
        remote(sent, sent, two_s.at[n], two_r.at[n], ring(1)).wait_send()


def hand_on(a, b, c, a_out, b_out, c_out):
    a_out[...], b_out[...], c_out[...] = a[...], b[...], c[...]


def body(field, wind, w_in, w_mid, w_out, targets, column_map, batch_count):
    vmem = pl.BlockSpec(memory_space=pltpu.VMEM)
    hbm = pl.BlockSpec(memory_space=pltpu.HBM)
    hid = w_mid.shape[0]
    dma = pltpu.SemaphoreType.DMA
    V = pltpu.VMEM
    results = pl.pallas_call(
        kernel,
        out_shape=(
            jax.ShapeDtypeStruct((4, 32, LANES), f32),
            jax.ShapeDtypeStruct((16, hid), f32),
            jax.ShapeDtypeStruct((16, LANES), f32),
        ),
        in_specs=[hbm] * 8,
        out_specs=(vmem, vmem, vmem),
        scratch_shapes=[
            V((1, LANES), jnp.int32),
            V((1, 32), jnp.int32),
            V((8, 48, LANES), f32),
            V((6, 48, LANES), f32),
            V((4, hid, WIDE), bf16),
            V((LANES, hid), bf16),
            V((hid, LANES), bf16),
            V((hid, LANES), bf16),
            V((LANES, LANES), f32),
            V((LANES, hid), bf16),
            V((hid, RANKS * LANES), bf16),
            V((LANES, hid), bf16),
            V((LANES, hid), f32),
            V((RANKS * LANES, LANES), bf16),
            V((6, 48, LANES), f32),
            V((2, RANKS, LANES, LANES), bf16),
            V((2, RANKS * LANES, LANES), bf16),
            V((8, LANES), f32),
            V((RANKS, 8, LANES), f32),
            V((8, LANES), f32),
            V((SIDE * SIDE, 8, LANES), f32),
            V((3, 4, SIDE, SIDE, 32, LANES), bf16),
            V((3, 2, SIDE, 2, SIDE, 32, LANES), bf16),
            V((2, SIDE, 2, 2, 1, 16, LANES), bf16),
            V((2, SIDE, 2, 2, 2, 16, LANES), bf16),
            V((SIDE * RANKS, 1, 16, LANES), bf16),
            V((SIDE * RANKS, 2, 16, LANES), bf16),
            dma((7,)),
            dma((4,)),
            dma((12,)),
            dma((12,)),
            dma((RANKS,)),
            dma((RANKS,)),
            dma((RANKS,)),
            dma((RANKS,)),
            dma((SIDE * SIDE,)),
            dma((SIDE * SIDE,)),
            dma((2, RANKS)),
            dma((2, RANKS)),
            dma((3, 2, SIDE)),
            dma((3, 2, SIDE)),
            dma((2,)),
            dma((2,)),
            pltpu.SemaphoreType.REGULAR((2,)),
        ],
        compiler_params=pltpu.CompilerParams(
            collective_id=0, has_side_effects=True, vmem_limit_bytes=VMEM_BYTES
        ),
        cost_estimate=pl.CostEstimate(
            flops=3_000_000_000, bytes_accessed=12_000_000, transcendentals=3_000_000
        ),
    )(
        field,
        wind,
        w_in,
        w_mid,
        w_out,
        targets,
        column_map.reshape(1, LANES),
        batch_count.reshape(1, 32),
    )
    return pl.pallas_call(
        hand_on,
        out_shape=tuple(jax.ShapeDtypeStruct(r.shape, r.dtype) for r in results),
        in_specs=[vmem] * 3,
        out_specs=(vmem,) * 3,
        compiler_params=pltpu.CompilerParams(vmem_limit_bytes=VMEM_BYTES),
    )(*results)


def solution(mesh):
    placed = (
        P("grp", "lon", None),
        P("grp", "lon", None),
        P(),
        P(),
        P(),
        P("lon", None),
        P("grp", "lon", None, None),
        P(),
    )
    return jax.shard_map(
        body,
        mesh=mesh,
        in_specs=placed,
        out_specs=(P("grp", "lon", None), P(("grp", "lon"), None), P(("grp", "lon"), None)),
        check_vma=False,
    )
```

```python
import jax
import jax.numpy as jnp
from jax import lax
from jax.experimental import pallas as pl
from jax.experimental.pallas import tpu as pltpu
from jax.sharding import PartitionSpec as P

MESH = pl.DeviceIdType.MESH
bf16, f32 = jnp.bfloat16, jnp.float32

LOSS_SCALE = 1024.0
PHYSICS_SHARE = 0.5
RANKS = 8
SIDE = 4
LANES = 128
VMEM_BYTES = 62 * 1024 * 1024
BLOCK = 256
WIDE = 512
NT = (((1,), (1,)), ((), ()))
TN = (((0,), (0,)), ((), ()))


def sigmoid(v):
    return 0.5 + 0.5 * jnp.tanh(0.5 * v)


def wide(i, size):
    return pl.ds(pl.multiple_of(i * size, size), size)


def kernel(
    field, wind, w_in, w_mid, w_out, targets, cmap_in, batch_in,
    field_out, grad_mid, grad_out,
    cmap, batch, ext, mids, win, wint, wout, goal, first, firsts, second, slope, inputs,
    step, outgoing, mine, cnt_out, cnt_in, sum_out, sum_in,
    part, got_one, half_0, half_1, got_0, got_1,
    load_sem, mid_sem, halo_s, halo_r, in_s, in_r, cnt_s, cnt_r, sum_s, sum_r,
    m_s, m_r, one_s, one_r, two_s, two_r, passed,
):
    grp, lon = lax.axis_index("grp"), lax.axis_index("lon")
    place, zh = lax.div(lon, 2), lax.rem(lon, 2)
    x, y = lax.div(place, SIDE), lax.rem(place, SIDE)
    rank = zh * 4 + grp
    is_trainer = grp == 3

    def rank_at(k):
        return lax.rem(rank + k, RANKS)

    def ring(k):
        other = rank_at(k)
        return (lax.rem(other, 4), place * 2 + lax.div(other, 4))

    def plane(k):
        return (grp, lax.rem(place + k, SIDE * SIDE) * 2 + zh)

    def along_x(k):
        return (grp, lax.rem(x + k, SIDE) * (2 * SIDE) + y * 2 + zh)

    def along_y(k):
        return (grp, x * (2 * SIDE) + lax.rem(y + k, SIDE) * 2 + zh)

    def beside(dg, dl):
        return (lax.rem(grp + dg + 4, 4), lax.rem(lon + dl + 32, 32))

    def remote(src, dst, send, recv, to):
        return pltpu.make_async_remote_copy(
            src_ref=src, dst_ref=dst, send_sem=send, recv_sem=recv,
            device_id=to, device_id_type=MESH,
        )

    loads = [
        pltpu.make_async_copy(field, ext.at[0, 2:6, 8:40], load_sem.at[0]),
        pltpu.make_async_copy(w_in, win, load_sem.at[1]),
        pltpu.make_async_copy(wind, ext.at[1, 2:6, 8:40], load_sem.at[2]),
        pltpu.make_async_copy(w_out, wout, load_sem.at[3]),
        pltpu.make_async_copy(targets, goal, load_sem.at[4]),
        pltpu.make_async_copy(cmap_in, cmap, load_sem.at[5]),
        pltpu.make_async_copy(batch_in, batch, load_sem.at[6]),
    ]

    def mid_load(c):
        return pltpu.make_async_copy(w_mid.at[:, c * WIDE : c * WIDE + WIDE], mids.at[c], mid_sem.at[c])

    barrier = pltpu.get_barrier_semaphore()
    far = 2 * zh - 1
    x_peers, y_peers = [along_x(k) for k in range(1, SIDE)], [along_y(k) for k in range(1, SIDE)]
    greeted = [ring(k) for k in range(1, RANKS)] + x_peers + y_peers
    for other in greeted:
        pl.semaphore_signal(barrier, inc=1, device_id=other, device_id_type=MESH)

    for i in (0, 2, 5, 1, 3):
        loads[i].start()
    for c in range(4):
        mid_load(c).start()
    for i in (4, 6):
        loads[i].start()

    loads[5].wait()
    names = jnp.broadcast_to(cmap[...].astype(f32), (LANES, LANES)).T
    ids = lax.broadcasted_iota(jnp.int32, (LANES, LANES), 1).astype(f32)
    match = (names == ids).astype(f32)
    own_count = jnp.sum(match, 0, keepdims=True) * jnp.where(is_trainer, 0.0, 1.0)
    cnt_out[...] = jnp.broadcast_to(own_count, (8, LANES))

    loads[0].wait()
    own_in = ext[0, 2:6, 8:40].reshape(LANES, LANES).astype(bf16)
    inputs[wide(rank, LANES), :] = own_in
    loads[2].wait()
    pl.semaphore_wait(barrier, len(greeted))

    in_copies = [
        remote(
            inputs.at[wide(rank, LANES)], inputs.at[wide(rank, LANES)],
            in_s.at[k], in_r.at[k], ring(k),
        ) for k in range(1, RANKS)
    ]
    cnt_copies = [
        remote(cnt_out, cnt_in.at[k], cnt_s.at[k], cnt_r.at[k], ring(k)) for k in range(1, RANKS)
    ]
    def edge(dl):
        return pl.ds(pl.multiple_of(20 + 12 * dl, 8), 8)

    def rim(dl):
        return pl.ds(pl.multiple_of(20 - 20 * dl, 8), 8)

    halo = [
        (ext.at[:, 2:4, 8:40], ext.at[:, 6:8, 8:40], -1, 0),
        (ext.at[:, 4:6, 8:40], ext.at[:, 0:2, 8:40], 1, 0),
    ]
    for dl in (-far, far):
        halo += [
            (ext.at[:, 2:6, edge(dl)], ext.at[:, 2:6, rim(dl)], 0, dl),
            (ext.at[0, 2, edge(dl)], ext.at[0, 6, rim(dl)], -1, dl),
            (ext.at[0, 5, edge(dl)], ext.at[0, 1, rim(dl)], 1, dl),
        ]
    halo_copies = [
        remote(src, dst, halo_s.at[i], halo_r.at[i], beside(dg, dl))
        for i, (src, dst, dg, dl) in enumerate(halo)
    ]
    for copy in cnt_copies:
        copy.start()
    for other in x_peers + y_peers:
        pl.semaphore_signal(passed.at[0], inc=1, device_id=other, device_id_type=MESH)
    for copy in halo_copies[:5] + in_copies:
        copy.start()

    loads[1].wait()
    own_in = inputs[wide(rank, LANES), :]

    for c in range(4):
        pre = jnp.dot(own_in, win[:, c * 512 : c * 512 + 512], preferred_element_type=f32)
        first[:, c * 512 : c * 512 + 512] = (pre * sigmoid(pre)).astype(bf16)
    loads[3].wait()

    def second_step(c):
        mid_load(c).wait()
        at = slice(c * WIDE, c * WIDE + WIDE)
        pre = jnp.dot(first[...], mids[c], preferred_element_type=f32)
        sig = sigmoid(pre)
        act = (pre * sig).astype(bf16)
        second[:, at] = act
        slope[:, at] = sig * (1.0 + pre * (1.0 - sig))
        return jnp.dot(act, wout[at, :], preferred_element_type=f32)

    pl.semaphore_wait(passed.at[0], len(x_peers) + len(y_peers))
    for other in x_peers:
        pl.semaphore_signal(passed.at[1], inc=1, device_id=other, device_id_type=MESH)
    predicted = second_step(0)
    pl.semaphore_wait(passed.at[1], len(x_peers))
    for copy in halo_copies[5:]:
        copy.start()

    total = cnt_out[...]
    for k in range(1, RANKS):
        cnt_copies[k - 1].wait_recv()
        total = total + cnt_in[k]
    sum_out[...] = total
    sum_copies = [
        remote(sum_out, sum_in.at[k], sum_s.at[k], sum_r.at[k], plane(k))
        for k in range(1, SIDE * SIDE)
    ]
    for copy in sum_copies:
        copy.start()

    for c in range(1, 4):
        predicted = predicted + second_step(c)

    def turn_step(c, carry):
        wint[wide(c, BLOCK), :] = win[:, wide(c, BLOCK)].T
        return carry

    lax.fori_loop(0, RANKS, turn_step, 0)

    for copy in halo_copies:
        copy.wait_recv()
    low, high = grp == 0, grp == 2

    def masked(row, values):
        if row < 0:
            return jnp.where(low, 0.0, values)
        if row > 3:
            return jnp.where(high, 0.0, values)
        return values

    def advanced(c, n, s, e, w, u):
        return c - 0.25 * u * (e - w) + 0.15 * (e + w + n + s - 4.0 * c)

    for row in range(-1, 5):
        i = row + 2
        c = masked(row, ext[0, i, 7:41])
        e, w = masked(row, ext[0, i, 8:42]), masked(row, ext[0, i, 6:40])
        n, s = masked(row + 1, ext[0, i + 1, 7:41]), masked(row - 1, ext[0, i - 1, 7:41])
        step[row + 1, 7:41] = masked(row, advanced(c, n, s, e, w, ext[1, i, 7:41]))
    current = []
    for row in range(4):
        c = step[row + 1, 8:40]
        e, w = step[row + 1, 9:41], step[row + 1, 7:39]
        n, s = step[row + 2, 8:40], step[row, 8:40]
        current.append(advanced(c, n, s, e, w, ext[1, row + 2, 8:40]))
    current = jnp.concatenate(current, 0)
    start = ext[0, 2:6, 8:40].reshape(LANES, LANES)
    increment = (current - start).astype(bf16).astype(f32)
    loads[4].wait()
    wanted = jnp.where(is_trainer, goal[...], increment)

    total = sum_out[...]
    for k in range(1, SIDE * SIDE):
        sum_copies[k - 1].wait_recv()
        total = total + sum_in[k]
    loads[6].wait()
    valid = batch[...].astype(f32)
    weight = LOSS_SCALE / (32.0 * (valid + total[0:1, 0:32]))
    column_weight = jnp.sum(match[:, 0:32] * weight, 1, keepdims=True)
    own = lax.broadcasted_iota(jnp.int32, (1, 32), 1) == lon
    own_weight = jnp.sum(jnp.where(own, weight, 0.0), 1, keepdims=True)
    own_valid = jnp.sum(jnp.where(own, valid, 0.0), 1, keepdims=True)
    rows = lax.broadcasted_iota(jnp.int32, (LANES, 1), 0).astype(f32)
    replay_weight = jnp.where(rows < own_valid, own_weight, 0.0)
    row_weight = jnp.where(is_trainer, replay_weight, column_weight)

    tendency = predicted.astype(bf16).astype(f32)
    sim = current + PHYSICS_SHARE * tendency
    field_out[...] = jnp.where(is_trainer, predicted, sim).reshape(4, 32, LANES)
    out_slope = ((predicted - wanted) * row_weight).astype(bf16)

    def m_copy(k, h):
        return remote(
            outgoing.at[h, rank_at(k)], mine.at[h, wide(rank, LANES)],
            m_s.at[h, k], m_r.at[h, k], ring(k),
        )

    for group in ((4, 3, 5, 2), (6, 1, 7, 0)):
        for k in group:
            t = rank_at(k)
            back = lax.dot_general(
                out_slope, wout[wide(t, BLOCK), :], NT, preferred_element_type=f32
            )
            value = (back * slope[:, wide(t, BLOCK)]).astype(bf16)
            outgoing[0, t] = value[:, :LANES]
            outgoing[1, t] = value[:, LANES:]
        for k in group:
            if k:
                m_copy(k, 0).start()
    for k in (4, 3, 5, 2, 6, 1, 7):
        m_copy(k, 1).start()
    for h in range(2):
        mine[h, wide(rank, LANES), :] = outgoing[h, rank]

    def one_copy(q, k, g):
        if g < 2:
            src, to = part.at[q, g, lax.rem(x + k, SIDE)], along_x(k)
        else:
            src, to = part.at[q, g, :, lax.rem(y + k, SIDE)], along_y(k)
        axis = g // 2
        return remote(
            src, got_one.at[q, axis, k, g % 2], one_s.at[q, axis, k], one_r.at[q, axis, k], to
        )

    def one_pair(q, axis, k):
        both = got_one.at[q, axis, k]
        return remote(both, both, one_s.at[q, axis, k], one_r.at[q, axis, k], along_x(k))

    halves, gots = (half_0, half_1), (got_0, got_1)

    def out_copy(n, axis, k, g, z):
        if axis == 0:
            at = lax.rem(y + k, SIDE)
            lon_at = x * (2 * SIDE) + at * 2 + z
        else:
            at = lax.rem(x + k, SIDE)
            lon_at = at * (2 * SIDE) + y * 2 + z
        src, dst = halves[n].at[axis, at, g, z], gots[n].at[k * RANKS + rank]
        return remote(src, dst, two_s.at[n], two_r.at[n], (2 * axis + g, lon_at))

    def own_copy(n, axis, g, z):
        src = halves[n].at[axis, y if axis == 0 else x, g, z]
        return pltpu.make_async_copy(src, gots[n].at[rank], two_r.at[n])

    def send_out(n, axis):
        rows = [(g, z) for g in range(2) for z in range(2)]
        for k in (2, 1, 3):
            for g, z in rows:
                out_copy(n, axis, k, g, z).start()
        for g, z in rows:
            here = (grp == 2 * axis + g) & (zh == z)

            @pl.when(here)
            def _():
                own_copy(n, axis, g, z).start()

            @pl.when(jnp.logical_not(here))
            def _():
                out_copy(n, axis, 0, g, z).start()

    def out_all(n):
        return remote(gots[n], gots[n], two_s.at[n], two_r.at[n], ring(1))

    def make_part(q, product):
        for g in (0, 2, 1, 3):
            part[q, g] = product(g).astype(bf16).reshape(SIDE, SIDE, 32, LANES)
            for k in (2, 1, 3):
                one_copy(q, k, g).start()

    def reduce_one(n, parts):
        for axis in range(2):
            for i, q in enumerate(parts):
                total = part[q, 0:2, x] if axis == 0 else part[q, 2:4, :, y]
                total = total.astype(f32)
                for k in range(1, SIDE):
                    one_pair(q, axis, k).wait_recv()
                    total = total + got_one[q, axis, k].astype(f32)
                total = total.astype(bf16).reshape(2, SIDE, 2, 16, LANES)
                for g in range(2):
                    halves[n][axis, :, g, :, i] = total[g]
            send_out(n, axis)

    make_part(
        0,
        lambda g: lax.dot_general(
            second[:, g * 512 : g * 512 + 512], out_slope, TN, preferred_element_type=f32
        ),
    )

    for copy in in_copies:
        copy.wait_recv()

    def firsts_step(i, carry):
        c, n = lax.div(i, 2), lax.rem(i, 2)
        pre = lax.dot_general(
            wint[wide(c, BLOCK), :], inputs[wide(n, 512), :], NT, preferred_element_type=f32
        )
        firsts[wide(c, BLOCK), wide(n, 512)] = (pre * sigmoid(pre)).astype(bf16)
        return carry

    lax.fori_loop(0, 2 * RANKS, firsts_step, 0, unroll=2)

    for h in range(2):
        for k in range(1, RANKS):
            m_copy(k, h).wait_recv()
        make_part(
            1 + h,
            lambda g: jnp.dot(
                firsts[g * 512 : g * 512 + 512, :], mine[h], preferred_element_type=f32
            ),
        )
    reduce_one(0, (0,))
    for copy in in_copies + cnt_copies + halo_copies + sum_copies:
        copy.wait_send()
    for h in range(2):
        for k in range(1, RANKS):
            m_copy(k, h).wait_send()
    reduce_one(1, (1, 2))
    for q in range(3):
        for k in range(1, SIDE):
            for axis in range(2):
                one_pair(q, axis, k).wait_send()

    out_all(0).wait_recv()
    grad_out[...] = jnp.sum(got_0[:, 0].astype(f32), 0)
    out_all(1).wait_recv()
    for h in range(2):
        total = jnp.sum(got_1[:, h].astype(f32).reshape(SIDE, RANKS, 16, LANES), 0)
        for t in range(RANKS):
            at = t * BLOCK + h * LANES
            grad_mid[:, at : at + LANES] = total[t]

    for n in range(2):
        sent = gots[n].at[1:]
        remote(sent, sent, two_s.at[n], two_r.at[n], ring(1)).wait_send()


def hand_on(a, b, c, a_out, b_out, c_out):
    a_out[...], b_out[...], c_out[...] = a[...], b[...], c[...]


def body(field, wind, w_in, w_mid, w_out, targets, column_map, batch_count):
    vmem = pl.BlockSpec(memory_space=pltpu.VMEM)
    hbm = pl.BlockSpec(memory_space=pltpu.HBM)
    hid = w_mid.shape[0]
    dma = pltpu.SemaphoreType.DMA
    V = pltpu.VMEM
    results = pl.pallas_call(
        kernel,
        out_shape=(
            jax.ShapeDtypeStruct((4, 32, LANES), f32),
            jax.ShapeDtypeStruct((16, hid), f32),
            jax.ShapeDtypeStruct((16, LANES), f32),
        ),
        in_specs=[hbm] * 8,
        out_specs=(vmem, vmem, vmem),
        scratch_shapes=[
            V((1, LANES), jnp.int32),
            V((1, 32), jnp.int32),
            V((2, 8, 48, LANES), f32),
            V((4, hid, WIDE), bf16),
            V((LANES, hid), bf16),
            V((hid, LANES), bf16),
            V((hid, LANES), bf16),
            V((LANES, LANES), f32),
            V((LANES, hid), bf16),
            V((hid, RANKS * LANES), bf16),
            V((LANES, hid), bf16),
            V((LANES, hid), f32),
            V((RANKS * LANES, LANES), bf16),
            V((6, 48, LANES), f32),
            V((2, RANKS, LANES, LANES), bf16),
            V((2, RANKS * LANES, LANES), bf16),
            V((8, LANES), f32),
            V((RANKS, 8, LANES), f32),
            V((8, LANES), f32),
            V((SIDE * SIDE, 8, LANES), f32),
            V((3, 4, SIDE, SIDE, 32, LANES), bf16),
            V((3, 2, SIDE, 2, SIDE, 32, LANES), bf16),
            V((2, SIDE, 2, 2, 1, 16, LANES), bf16),
            V((2, SIDE, 2, 2, 2, 16, LANES), bf16),
            V((SIDE * RANKS, 1, 16, LANES), bf16),
            V((SIDE * RANKS, 2, 16, LANES), bf16),
            dma((7,)),
            dma((4,)),
            dma((8,)),
            dma((8,)),
            dma((RANKS,)),
            dma((RANKS,)),
            dma((RANKS,)),
            dma((RANKS,)),
            dma((SIDE * SIDE,)),
            dma((SIDE * SIDE,)),
            dma((2, RANKS)),
            dma((2, RANKS)),
            dma((3, 2, SIDE)),
            dma((3, 2, SIDE)),
            dma((2,)),
            dma((2,)),
            pltpu.SemaphoreType.REGULAR((2,)),
        ],
        compiler_params=pltpu.CompilerParams(
            collective_id=0, has_side_effects=True, vmem_limit_bytes=VMEM_BYTES
        ),
        cost_estimate=pl.CostEstimate(
            flops=3_000_000_000, bytes_accessed=12_000_000, transcendentals=3_000_000
        ),
    )(
        field,
        wind,
        w_in,
        w_mid,
        w_out,
        targets,
        column_map.reshape(1, LANES),
        batch_count.reshape(1, 32),
    )
    return pl.pallas_call(
        hand_on,
        out_shape=tuple(jax.ShapeDtypeStruct(r.shape, r.dtype) for r in results),
        in_specs=[vmem] * 3,
        out_specs=(vmem,) * 3,
        compiler_params=pltpu.CompilerParams(vmem_limit_bytes=VMEM_BYTES),
    )(*results)


def solution(mesh):
    placed = (
        P("grp", "lon", None),
        P("grp", "lon", None),
        P(),
        P(),
        P(),
        P("lon", None),
        P("grp", "lon", None, None),
        P(),
    )
    return jax.shard_map(
        body,
        mesh=mesh,
        in_specs=placed,
        out_specs=(P("grp", "lon", None), P(("grp", "lon"), None), P(("grp", "lon"), None)),
        check_vma=False,
    )
```

```python
import jax
import jax.numpy as jnp
from jax import lax
from jax.experimental import pallas as pl
from jax.experimental.pallas import tpu as pltpu
from jax.sharding import PartitionSpec as P

MESH = pl.DeviceIdType.MESH
bf16, f32 = jnp.bfloat16, jnp.float32

LOSS_SCALE = 1024.0
PHYSICS_SHARE = 0.5
RANKS = 8
SIDE = 4
LANES = 128
VMEM_BYTES = 62 * 1024 * 1024
BLOCK = 256
WIDE = 512
NT = (((1,), (1,)), ((), ()))
TN = (((0,), (0,)), ((), ()))


def sigmoid(v):
    return 0.5 + 0.5 * jnp.tanh(0.5 * v)


def wide(i, size):
    return pl.ds(pl.multiple_of(i * size, size), size)


def kernel(
    field, wind, w_in, w_mid, w_out, targets, cmap_in, batch_in,
    field_out, grad_mid, grad_out,
    cmap, batch, ext, mids, win, wint, wout, goal, first, firsts, second, slope, inputs,
    step, outgoing, mine, cnt_out, cnt_in, sum_out, sum_in,
    part, got_one, half_0, half_1, got_0, got_1,
    load_sem, mid_sem, halo_s, halo_r, in_s, in_r, cnt_s, cnt_r, sum_s, sum_r,
    m_s, m_r, one_s, one_r, two_s, two_r, passed,
):
    grp, lon = lax.axis_index("grp"), lax.axis_index("lon")
    place, zh = lax.div(lon, 2), lax.rem(lon, 2)
    x, y = lax.div(place, SIDE), lax.rem(place, SIDE)
    rank = zh * 4 + grp
    is_trainer = grp == 3

    def rank_at(k):
        return lax.rem(rank + k, RANKS)

    def ring(k):
        other = rank_at(k)
        return (lax.rem(other, 4), place * 2 + lax.div(other, 4))

    def plane(k):
        return (grp, lax.rem(place + k, SIDE * SIDE) * 2 + zh)

    def along_x(k):
        return (grp, lax.rem(x + k, SIDE) * (2 * SIDE) + y * 2 + zh)

    def along_y(k):
        return (grp, x * (2 * SIDE) + lax.rem(y + k, SIDE) * 2 + zh)

    def beside(dg, dl):
        return (lax.rem(grp + dg + 4, 4), lax.rem(lon + dl + 32, 32))

    def remote(src, dst, send, recv, to):
        return pltpu.make_async_remote_copy(
            src_ref=src, dst_ref=dst, send_sem=send, recv_sem=recv,
            device_id=to, device_id_type=MESH,
        )

    loads = [
        pltpu.make_async_copy(field, ext.at[0, 2:6, 8:40], load_sem.at[0]),
        pltpu.make_async_copy(w_in, win, load_sem.at[1]),
        pltpu.make_async_copy(wind, ext.at[1, 2:6, 8:40], load_sem.at[2]),
        pltpu.make_async_copy(w_out, wout, load_sem.at[3]),
        pltpu.make_async_copy(targets, goal, load_sem.at[4]),
        pltpu.make_async_copy(cmap_in, cmap, load_sem.at[5]),
        pltpu.make_async_copy(batch_in, batch, load_sem.at[6]),
    ]

    def mid_load(c):
        return pltpu.make_async_copy(w_mid.at[:, c * WIDE : c * WIDE + WIDE], mids.at[c], mid_sem.at[c])

    barrier = pltpu.get_barrier_semaphore()
    far = 2 * zh - 1
    x_peers, y_peers = [along_x(k) for k in range(1, SIDE)], [along_y(k) for k in range(1, SIDE)]
    greeted = [ring(k) for k in range(1, RANKS)] + x_peers + y_peers
    for other in greeted:
        pl.semaphore_signal(barrier, inc=1, device_id=other, device_id_type=MESH)

    for i in (5, 0, 2, 1, 3):
        loads[i].start()
    for c in range(4):
        mid_load(c).start()
    for i in (4, 6):
        loads[i].start()

    loads[5].wait()
    names = jnp.broadcast_to(cmap[...].astype(f32), (LANES, LANES)).T
    ids = lax.broadcasted_iota(jnp.int32, (LANES, LANES), 1).astype(f32)
    match = (names == ids).astype(f32)
    own_count = jnp.sum(match, 0, keepdims=True) * jnp.where(is_trainer, 0.0, 1.0)
    cnt_out[...] = jnp.broadcast_to(own_count, (8, LANES))

    pl.semaphore_wait(barrier, len(greeted))

    in_copies = [
        remote(
            inputs.at[wide(rank, LANES)], inputs.at[wide(rank, LANES)],
            in_s.at[k], in_r.at[k], ring(k),
        ) for k in range(1, RANKS)
    ]
    cnt_copies = [
        remote(cnt_out, cnt_in.at[k], cnt_s.at[k], cnt_r.at[k], ring(k)) for k in range(1, RANKS)
    ]
    def edge(dl):
        return pl.ds(pl.multiple_of(20 + 12 * dl, 8), 8)

    def rim(dl):
        return pl.ds(pl.multiple_of(20 - 20 * dl, 8), 8)

    halo = [
        (ext.at[:, 2:4, 8:40], ext.at[:, 6:8, 8:40], -1, 0),
        (ext.at[:, 4:6, 8:40], ext.at[:, 0:2, 8:40], 1, 0),
    ]
    for dl in (-far, far):
        halo += [
            (ext.at[:, 2:6, edge(dl)], ext.at[:, 2:6, rim(dl)], 0, dl),
            (ext.at[0, 2, edge(dl)], ext.at[0, 6, rim(dl)], -1, dl),
            (ext.at[0, 5, edge(dl)], ext.at[0, 1, rim(dl)], 1, dl),
        ]
    halo_copies = [
        remote(src, dst, halo_s.at[i], halo_r.at[i], beside(dg, dl))
        for i, (src, dst, dg, dl) in enumerate(halo)
    ]
    for copy in cnt_copies:
        copy.start()
    for other in x_peers + y_peers:
        pl.semaphore_signal(passed.at[0], inc=1, device_id=other, device_id_type=MESH)
    loads[0].wait()
    own_in = ext[0, 2:6, 8:40].reshape(LANES, LANES).astype(bf16)
    inputs[wide(rank, LANES), :] = own_in
    loads[2].wait()
    for copy in halo_copies[:5] + in_copies:
        copy.start()

    pl.semaphore_wait(passed.at[0], len(x_peers) + len(y_peers))
    for other in x_peers:
        pl.semaphore_signal(passed.at[1], inc=1, device_id=other, device_id_type=MESH)

    loads[1].wait()
    own_in = inputs[wide(rank, LANES), :]

    for c in range(4):
        pre = jnp.dot(own_in, win[:, c * 512 : c * 512 + 512], preferred_element_type=f32)
        first[:, c * 512 : c * 512 + 512] = (pre * sigmoid(pre)).astype(bf16)
    loads[3].wait()

    def second_step(c):
        mid_load(c).wait()
        at = slice(c * WIDE, c * WIDE + WIDE)
        pre = jnp.dot(first[...], mids[c], preferred_element_type=f32)
        sig = sigmoid(pre)
        act = (pre * sig).astype(bf16)
        second[:, at] = act
        slope[:, at] = sig * (1.0 + pre * (1.0 - sig))
        return jnp.dot(act, wout[at, :], preferred_element_type=f32)

    predicted = second_step(0)
    pl.semaphore_wait(passed.at[1], len(x_peers))
    for copy in halo_copies[5:]:
        copy.start()

    total = cnt_out[...]
    for k in range(1, RANKS):
        cnt_copies[k - 1].wait_recv()
        total = total + cnt_in[k]
    sum_out[...] = total
    sum_copies = [
        remote(sum_out, sum_in.at[k], sum_s.at[k], sum_r.at[k], plane(k))
        for k in range(1, SIDE * SIDE)
    ]
    for copy in sum_copies:
        copy.start()

    for c in range(1, 4):
        predicted = predicted + second_step(c)

    def turn_step(c, carry):
        wint[wide(c, BLOCK), :] = win[:, wide(c, BLOCK)].T
        return carry

    lax.fori_loop(0, RANKS, turn_step, 0)

    for copy in halo_copies:
        copy.wait_recv()
    low, high = grp == 0, grp == 2

    def masked(row, values):
        if row < 0:
            return jnp.where(low, 0.0, values)
        if row > 3:
            return jnp.where(high, 0.0, values)
        return values

    def advanced(c, n, s, e, w, u):
        return c - 0.25 * u * (e - w) + 0.15 * (e + w + n + s - 4.0 * c)

    for row in range(-1, 5):
        i = row + 2
        c = masked(row, ext[0, i, 7:41])
        e, w = masked(row, ext[0, i, 8:42]), masked(row, ext[0, i, 6:40])
        n, s = masked(row + 1, ext[0, i + 1, 7:41]), masked(row - 1, ext[0, i - 1, 7:41])
        step[row + 1, 7:41] = masked(row, advanced(c, n, s, e, w, ext[1, i, 7:41]))
    current = []
    for row in range(4):
        c = step[row + 1, 8:40]
        e, w = step[row + 1, 9:41], step[row + 1, 7:39]
        n, s = step[row + 2, 8:40], step[row, 8:40]
        current.append(advanced(c, n, s, e, w, ext[1, row + 2, 8:40]))
    current = jnp.concatenate(current, 0)
    start = ext[0, 2:6, 8:40].reshape(LANES, LANES)
    increment = (current - start).astype(bf16).astype(f32)
    loads[4].wait()
    wanted = jnp.where(is_trainer, goal[...], increment)

    total = sum_out[...]
    for k in range(1, SIDE * SIDE):
        sum_copies[k - 1].wait_recv()
        total = total + sum_in[k]
    loads[6].wait()
    valid = batch[...].astype(f32)
    weight = LOSS_SCALE / (32.0 * (valid + total[0:1, 0:32]))
    column_weight = jnp.sum(match[:, 0:32] * weight, 1, keepdims=True)
    own = lax.broadcasted_iota(jnp.int32, (1, 32), 1) == lon
    own_weight = jnp.sum(jnp.where(own, weight, 0.0), 1, keepdims=True)
    own_valid = jnp.sum(jnp.where(own, valid, 0.0), 1, keepdims=True)
    rows = lax.broadcasted_iota(jnp.int32, (LANES, 1), 0).astype(f32)
    replay_weight = jnp.where(rows < own_valid, own_weight, 0.0)
    row_weight = jnp.where(is_trainer, replay_weight, column_weight)

    tendency = predicted.astype(bf16).astype(f32)
    sim = current + PHYSICS_SHARE * tendency
    field_out[...] = jnp.where(is_trainer, predicted, sim).reshape(4, 32, LANES)
    out_slope = ((predicted - wanted) * row_weight).astype(bf16)

    def m_copy(k, h):
        return remote(
            outgoing.at[h, rank_at(k)], mine.at[h, wide(rank, LANES)],
            m_s.at[h, k], m_r.at[h, k], ring(k),
        )

    for group in ((4, 3, 5, 2), (6, 1, 7, 0)):
        for k in group:
            t = rank_at(k)
            back = lax.dot_general(
                out_slope, wout[wide(t, BLOCK), :], NT, preferred_element_type=f32
            )
            value = (back * slope[:, wide(t, BLOCK)]).astype(bf16)
            outgoing[0, t] = value[:, :LANES]
            outgoing[1, t] = value[:, LANES:]
        for k in group:
            if k:
                m_copy(k, 0).start()
    for k in (4, 3, 5, 2, 6, 1, 7):
        m_copy(k, 1).start()
    for h in range(2):
        mine[h, wide(rank, LANES), :] = outgoing[h, rank]

    def one_copy(q, k, g):
        if g < 2:
            src, to = part.at[q, g, lax.rem(x + k, SIDE)], along_x(k)
        else:
            src, to = part.at[q, g, :, lax.rem(y + k, SIDE)], along_y(k)
        axis = g // 2
        return remote(
            src, got_one.at[q, axis, k, g % 2], one_s.at[q, axis, k], one_r.at[q, axis, k], to
        )

    def one_pair(q, axis, k):
        both = got_one.at[q, axis, k]
        return remote(both, both, one_s.at[q, axis, k], one_r.at[q, axis, k], along_x(k))

    halves, gots = (half_0, half_1), (got_0, got_1)

    def out_copy(n, axis, k, g, z):
        if axis == 0:
            at = lax.rem(y + k, SIDE)
            lon_at = x * (2 * SIDE) + at * 2 + z
        else:
            at = lax.rem(x + k, SIDE)
            lon_at = at * (2 * SIDE) + y * 2 + z
        src, dst = halves[n].at[axis, at, g, z], gots[n].at[k * RANKS + rank]
        return remote(src, dst, two_s.at[n], two_r.at[n], (2 * axis + g, lon_at))

    def own_copy(n, axis, g, z):
        src = halves[n].at[axis, y if axis == 0 else x, g, z]
        return pltpu.make_async_copy(src, gots[n].at[rank], two_r.at[n])

    def send_out(n, axis):
        rows = [(g, z) for g in range(2) for z in range(2)]
        for k in (2, 1, 3):
            for g, z in rows:
                out_copy(n, axis, k, g, z).start()
        for g, z in rows:
            here = (grp == 2 * axis + g) & (zh == z)

            @pl.when(here)
            def _():
                own_copy(n, axis, g, z).start()

            @pl.when(jnp.logical_not(here))
            def _():
                out_copy(n, axis, 0, g, z).start()

    def out_all(n):
        return remote(gots[n], gots[n], two_s.at[n], two_r.at[n], ring(1))

    def make_part(q, product):
        for g in (0, 2, 1, 3):
            part[q, g] = product(g).astype(bf16).reshape(SIDE, SIDE, 32, LANES)
            for k in (2, 1, 3):
                one_copy(q, k, g).start()

    def reduce_one(n, parts):
        for axis in range(2):
            for i, q in enumerate(parts):
                total = part[q, 0:2, x] if axis == 0 else part[q, 2:4, :, y]
                total = total.astype(f32)
                for k in range(1, SIDE):
                    one_pair(q, axis, k).wait_recv()
                    total = total + got_one[q, axis, k].astype(f32)
                total = total.astype(bf16).reshape(2, SIDE, 2, 16, LANES)
                for g in range(2):
                    halves[n][axis, :, g, :, i] = total[g]
            send_out(n, axis)

    make_part(
        0,
        lambda g: lax.dot_general(
            second[:, g * 512 : g * 512 + 512], out_slope, TN, preferred_element_type=f32
        ),
    )

    for copy in in_copies:
        copy.wait_recv()

    def firsts_step(i, carry):
        c, n = lax.div(i, 2), lax.rem(i, 2)
        pre = lax.dot_general(
            wint[wide(c, BLOCK), :], inputs[wide(n, 512), :], NT, preferred_element_type=f32
        )
        firsts[wide(c, BLOCK), wide(n, 512)] = (pre * sigmoid(pre)).astype(bf16)
        return carry

    lax.fori_loop(0, 2 * RANKS, firsts_step, 0, unroll=2)

    for h in range(2):
        for k in range(1, RANKS):
            m_copy(k, h).wait_recv()
        make_part(
            1 + h,
            lambda g: jnp.dot(
                firsts[g * 512 : g * 512 + 512, :], mine[h], preferred_element_type=f32
            ),
        )
    reduce_one(0, (0,))
    for copy in in_copies + cnt_copies + halo_copies + sum_copies:
        copy.wait_send()
    for h in range(2):
        for k in range(1, RANKS):
            m_copy(k, h).wait_send()
    reduce_one(1, (1, 2))
    for q in range(3):
        for k in range(1, SIDE):
            for axis in range(2):
                one_pair(q, axis, k).wait_send()

    out_all(0).wait_recv()
    grad_out[...] = jnp.sum(got_0[:, 0].astype(f32), 0)
    out_all(1).wait_recv()
    for h in range(2):
        total = jnp.sum(got_1[:, h].astype(f32).reshape(SIDE, RANKS, 16, LANES), 0)
        for t in range(RANKS):
            at = t * BLOCK + h * LANES
            grad_mid[:, at : at + LANES] = total[t]

    for n in range(2):
        sent = gots[n].at[1:]
        remote(sent, sent, two_s.at[n], two_r.at[n], ring(1)).wait_send()


def hand_on(a, b, c, a_out, b_out, c_out):
    a_out[...], b_out[...], c_out[...] = a[...], b[...], c[...]


def body(field, wind, w_in, w_mid, w_out, targets, column_map, batch_count):
    vmem = pl.BlockSpec(memory_space=pltpu.VMEM)
    hbm = pl.BlockSpec(memory_space=pltpu.HBM)
    hid = w_mid.shape[0]
    dma = pltpu.SemaphoreType.DMA
    V = pltpu.VMEM
    results = pl.pallas_call(
        kernel,
        out_shape=(
            jax.ShapeDtypeStruct((4, 32, LANES), f32),
            jax.ShapeDtypeStruct((16, hid), f32),
            jax.ShapeDtypeStruct((16, LANES), f32),
        ),
        in_specs=[hbm] * 8,
        out_specs=(vmem, vmem, vmem),
        scratch_shapes=[
            V((1, LANES), jnp.int32),
            V((1, 32), jnp.int32),
            V((2, 8, 48, LANES), f32),
            V((4, hid, WIDE), bf16),
            V((LANES, hid), bf16),
            V((hid, LANES), bf16),
            V((hid, LANES), bf16),
            V((LANES, LANES), f32),
            V((LANES, hid), bf16),
            V((hid, RANKS * LANES), bf16),
            V((LANES, hid), bf16),
            V((LANES, hid), f32),
            V((RANKS * LANES, LANES), bf16),
            V((6, 48, LANES), f32),
            V((2, RANKS, LANES, LANES), bf16),
            V((2, RANKS * LANES, LANES), bf16),
            V((8, LANES), f32),
            V((RANKS, 8, LANES), f32),
            V((8, LANES), f32),
            V((SIDE * SIDE, 8, LANES), f32),
            V((3, 4, SIDE, SIDE, 32, LANES), bf16),
            V((3, 2, SIDE, 2, SIDE, 32, LANES), bf16),
            V((2, SIDE, 2, 2, 1, 16, LANES), bf16),
            V((2, SIDE, 2, 2, 2, 16, LANES), bf16),
            V((SIDE * RANKS, 1, 16, LANES), bf16),
            V((SIDE * RANKS, 2, 16, LANES), bf16),
            dma((7,)),
            dma((4,)),
            dma((8,)),
            dma((8,)),
            dma((RANKS,)),
            dma((RANKS,)),
            dma((RANKS,)),
            dma((RANKS,)),
            dma((SIDE * SIDE,)),
            dma((SIDE * SIDE,)),
            dma((2, RANKS)),
            dma((2, RANKS)),
            dma((3, 2, SIDE)),
            dma((3, 2, SIDE)),
            dma((2,)),
            dma((2,)),
            pltpu.SemaphoreType.REGULAR((2,)),
        ],
        compiler_params=pltpu.CompilerParams(
            collective_id=0, has_side_effects=True, vmem_limit_bytes=VMEM_BYTES
        ),
        cost_estimate=pl.CostEstimate(
            flops=3_000_000_000, bytes_accessed=12_000_000, transcendentals=3_000_000
        ),
    )(
        field,
        wind,
        w_in,
        w_mid,
        w_out,
        targets,
        column_map.reshape(1, LANES),
        batch_count.reshape(1, 32),
    )
    return pl.pallas_call(
        hand_on,
        out_shape=tuple(jax.ShapeDtypeStruct(r.shape, r.dtype) for r in results),
        in_specs=[vmem] * 3,
        out_specs=(vmem,) * 3,
        compiler_params=pltpu.CompilerParams(vmem_limit_bytes=VMEM_BYTES),
    )(*results)


def solution(mesh):
    placed = (
        P("grp", "lon", None),
        P("grp", "lon", None),
        P(),
        P(),
        P(),
        P("lon", None),
        P("grp", "lon", None, None),
        P(),
    )
    return jax.shard_map(
        body,
        mesh=mesh,
        in_specs=placed,
        out_specs=(P("grp", "lon", None), P(("grp", "lon"), None), P(("grp", "lon"), None)),
        check_vma=False,
    )
```

```python
import jax
import jax.numpy as jnp
from jax import lax
from jax.experimental import pallas as pl
from jax.experimental.pallas import tpu as pltpu
from jax.sharding import PartitionSpec as P

MESH = pl.DeviceIdType.MESH
bf16, f32 = jnp.bfloat16, jnp.float32

LOSS_SCALE = 1024.0
PHYSICS_SHARE = 0.5
RANKS = 8
SIDE = 4
LANES = 128
VMEM_BYTES = 62 * 1024 * 1024
BLOCK = 256
WIDE = 512
NT = (((1,), (1,)), ((), ()))
TN = (((0,), (0,)), ((), ()))


def sigmoid(v):
    return 0.5 + 0.5 * jnp.tanh(0.5 * v)


def wide(i, size):
    return pl.ds(pl.multiple_of(i * size, size), size)


def kernel(
    field, wind, w_in, w_mid, w_out, targets, cmap_in, batch_in,
    field_out, grad_mid, grad_out,
    cmap, batch, ext, mids, win, wint, wout, goal, first, firsts, second, slope, inputs,
    step, outgoing, mine, cnt_out, cnt_in, sum_out, sum_in,
    part, got_one, half, got,
    load_sem, mid_sem, halo_s, halo_r, in_s, in_r, cnt_s, cnt_r, sum_s, sum_r,
    m_s, m_r, one_s, one_r, two_s, two_r, passed,
):
    grp, lon = lax.axis_index("grp"), lax.axis_index("lon")
    place, zh = lax.div(lon, 2), lax.rem(lon, 2)
    x, y = lax.div(place, SIDE), lax.rem(place, SIDE)
    rank = zh * 4 + grp
    is_trainer = grp == 3

    def rank_at(k):
        return lax.rem(rank + k, RANKS)

    def ring(k):
        other = rank_at(k)
        return (lax.rem(other, 4), place * 2 + lax.div(other, 4))

    def plane(k):
        return (grp, lax.rem(place + k, SIDE * SIDE) * 2 + zh)

    def along_x(k):
        return (grp, lax.rem(x + k, SIDE) * (2 * SIDE) + y * 2 + zh)

    def along_y(k):
        return (grp, x * (2 * SIDE) + lax.rem(y + k, SIDE) * 2 + zh)

    def beside(dg, dl):
        return (lax.rem(grp + dg + 4, 4), lax.rem(lon + dl + 32, 32))

    def remote(src, dst, send, recv, to):
        return pltpu.make_async_remote_copy(
            src_ref=src, dst_ref=dst, send_sem=send, recv_sem=recv,
            device_id=to, device_id_type=MESH,
        )

    loads = [
        pltpu.make_async_copy(field, ext.at[0, 2:6, 8:40], load_sem.at[0]),
        pltpu.make_async_copy(w_in, win, load_sem.at[1]),
        pltpu.make_async_copy(wind, ext.at[1, 2:6, 8:40], load_sem.at[2]),
        pltpu.make_async_copy(w_out, wout, load_sem.at[3]),
        pltpu.make_async_copy(targets, goal, load_sem.at[4]),
        pltpu.make_async_copy(cmap_in, cmap, load_sem.at[5]),
        pltpu.make_async_copy(batch_in, batch, load_sem.at[6]),
    ]

    def mid_load(c):
        return pltpu.make_async_copy(w_mid.at[:, c * WIDE : c * WIDE + WIDE], mids.at[c], mid_sem.at[c])

    barrier = pltpu.get_barrier_semaphore()
    far = 2 * zh - 1
    x_peers, y_peers = [along_x(k) for k in range(1, SIDE)], [along_y(k) for k in range(1, SIDE)]
    greeted = [ring(k) for k in range(1, RANKS)] + x_peers + y_peers
    for other in greeted:
        pl.semaphore_signal(barrier, inc=1, device_id=other, device_id_type=MESH)

    for i in (0, 2, 5, 1, 3):
        loads[i].start()
    for c in range(4):
        mid_load(c).start()
    for i in (4, 6):
        loads[i].start()

    loads[5].wait()
    names = jnp.broadcast_to(cmap[...].astype(f32), (LANES, LANES)).T
    ids = lax.broadcasted_iota(jnp.int32, (LANES, LANES), 1).astype(f32)
    match = (names == ids).astype(f32)
    own_count = jnp.sum(match, 0, keepdims=True) * jnp.where(is_trainer, 0.0, 1.0)
    cnt_out[...] = jnp.broadcast_to(own_count, (8, LANES))

    loads[0].wait()
    own_in = ext[0, 2:6, 8:40].reshape(LANES, LANES).astype(bf16)
    inputs[wide(rank, LANES), :] = own_in
    loads[2].wait()
    pl.semaphore_wait(barrier, len(greeted))

    in_copies = [
        remote(
            inputs.at[wide(rank, LANES)], inputs.at[wide(rank, LANES)],
            in_s.at[k], in_r.at[k], ring(k),
        ) for k in range(1, RANKS)
    ]
    cnt_copies = [
        remote(cnt_out, cnt_in.at[k], cnt_s.at[k], cnt_r.at[k], ring(k)) for k in range(1, RANKS)
    ]
    def edge(dl):
        return pl.ds(pl.multiple_of(20 + 12 * dl, 8), 8)

    def rim(dl):
        return pl.ds(pl.multiple_of(20 - 20 * dl, 8), 8)

    halo = [
        (ext.at[:, 2:4, 8:40], ext.at[:, 6:8, 8:40], -1, 0),
        (ext.at[:, 4:6, 8:40], ext.at[:, 0:2, 8:40], 1, 0),
    ]
    for dl in (-far, far):
        halo += [
            (ext.at[:, 2:6, edge(dl)], ext.at[:, 2:6, rim(dl)], 0, dl),
            (ext.at[0, 2, edge(dl)], ext.at[0, 6, rim(dl)], -1, dl),
            (ext.at[0, 5, edge(dl)], ext.at[0, 1, rim(dl)], 1, dl),
        ]
    halo_copies = [
        remote(src, dst, halo_s.at[i], halo_r.at[i], beside(dg, dl))
        for i, (src, dst, dg, dl) in enumerate(halo)
    ]
    for copy in cnt_copies:
        copy.start()
    for other in x_peers + y_peers:
        pl.semaphore_signal(passed.at[0], inc=1, device_id=other, device_id_type=MESH)
    for copy in halo_copies[:5] + in_copies:
        copy.start()

    loads[1].wait()
    own_in = inputs[wide(rank, LANES), :]

    for c in range(4):
        pre = jnp.dot(own_in, win[:, c * 512 : c * 512 + 512], preferred_element_type=f32)
        first[:, c * 512 : c * 512 + 512] = (pre * sigmoid(pre)).astype(bf16)
    loads[3].wait()

    def second_step(c):
        mid_load(c).wait()
        at = slice(c * WIDE, c * WIDE + WIDE)
        pre = jnp.dot(first[...], mids[c], preferred_element_type=f32)
        sig = sigmoid(pre)
        act = (pre * sig).astype(bf16)
        second[:, at] = act
        slope[:, at] = sig * (1.0 + pre * (1.0 - sig))
        return jnp.dot(act, wout[at, :], preferred_element_type=f32)

    pl.semaphore_wait(passed.at[0], len(x_peers) + len(y_peers))
    for other in x_peers:
        pl.semaphore_signal(passed.at[1], inc=1, device_id=other, device_id_type=MESH)
    predicted = second_step(0)
    pl.semaphore_wait(passed.at[1], len(x_peers))
    for copy in halo_copies[5:]:
        copy.start()

    total = cnt_out[...]
    for k in range(1, RANKS):
        cnt_copies[k - 1].wait_recv()
        total = total + cnt_in[k]
    sum_out[...] = total
    sum_copies = [
        remote(sum_out, sum_in.at[k], sum_s.at[k], sum_r.at[k], plane(k))
        for k in range(1, SIDE * SIDE)
    ]
    for copy in sum_copies:
        copy.start()

    for c in range(1, 4):
        predicted = predicted + second_step(c)

    def turn_step(c, carry):
        wint[wide(c, BLOCK), :] = win[:, wide(c, BLOCK)].T
        return carry

    lax.fori_loop(0, RANKS, turn_step, 0)

    for copy in halo_copies:
        copy.wait_recv()
    low, high = grp == 0, grp == 2

    def masked(row, values):
        if row < 0:
            return jnp.where(low, 0.0, values)
        if row > 3:
            return jnp.where(high, 0.0, values)
        return values

    def advanced(c, n, s, e, w, u):
        return c - 0.25 * u * (e - w) + 0.15 * (e + w + n + s - 4.0 * c)

    for row in range(-1, 5):
        i = row + 2
        c = masked(row, ext[0, i, 7:41])
        e, w = masked(row, ext[0, i, 8:42]), masked(row, ext[0, i, 6:40])
        n, s = masked(row + 1, ext[0, i + 1, 7:41]), masked(row - 1, ext[0, i - 1, 7:41])
        step[row + 1, 7:41] = masked(row, advanced(c, n, s, e, w, ext[1, i, 7:41]))
    current = []
    for row in range(4):
        c = step[row + 1, 8:40]
        e, w = step[row + 1, 9:41], step[row + 1, 7:39]
        n, s = step[row + 2, 8:40], step[row, 8:40]
        current.append(advanced(c, n, s, e, w, ext[1, row + 2, 8:40]))
    current = jnp.concatenate(current, 0)
    start = ext[0, 2:6, 8:40].reshape(LANES, LANES)
    increment = (current - start).astype(bf16).astype(f32)
    loads[4].wait()
    wanted = jnp.where(is_trainer, goal[...], increment)

    total = sum_out[...]
    for k in range(1, SIDE * SIDE):
        sum_copies[k - 1].wait_recv()
        total = total + sum_in[k]
    loads[6].wait()
    valid = batch[...].astype(f32)
    weight = LOSS_SCALE / (32.0 * (valid + total[0:1, 0:32]))
    column_weight = jnp.sum(match[:, 0:32] * weight, 1, keepdims=True)
    own = lax.broadcasted_iota(jnp.int32, (1, 32), 1) == lon
    own_weight = jnp.sum(jnp.where(own, weight, 0.0), 1, keepdims=True)
    own_valid = jnp.sum(jnp.where(own, valid, 0.0), 1, keepdims=True)
    rows = lax.broadcasted_iota(jnp.int32, (LANES, 1), 0).astype(f32)
    replay_weight = jnp.where(rows < own_valid, own_weight, 0.0)
    row_weight = jnp.where(is_trainer, replay_weight, column_weight)

    tendency = predicted.astype(bf16).astype(f32)
    sim = current + PHYSICS_SHARE * tendency
    field_out[...] = jnp.where(is_trainer, predicted, sim).reshape(4, 32, LANES)
    out_slope = ((predicted - wanted) * row_weight).astype(bf16)

    def m_copy(k, h):
        return remote(
            outgoing.at[h, rank_at(k)], mine.at[h, wide(rank, LANES)],
            m_s.at[h, k], m_r.at[h, k], ring(k),
        )

    for group in ((4, 3, 5, 2), (6, 1, 7, 0)):
        for k in group:
            t = rank_at(k)
            back = lax.dot_general(
                out_slope, wout[wide(t, BLOCK), :], NT, preferred_element_type=f32
            )
            value = (back * slope[:, wide(t, BLOCK)]).astype(bf16)
            outgoing[0, t] = value[:, :LANES]
            outgoing[1, t] = value[:, LANES:]
        for k in group:
            if k:
                m_copy(k, 0).start()
    for k in (4, 3, 5, 2, 6, 1, 7):
        m_copy(k, 1).start()
    for h in range(2):
        mine[h, wide(rank, LANES), :] = outgoing[h, rank]

    def one_copy(q, k, g):
        if g < 2:
            src, to = part.at[q, g, lax.rem(x + k, SIDE)], along_x(k)
        else:
            src, to = part.at[q, g, :, lax.rem(y + k, SIDE)], along_y(k)
        axis = g // 2
        return remote(
            src, got_one.at[q, axis, k, g % 2], one_s.at[q, axis, k], one_r.at[q, axis, k], to
        )

    def one_pair(q, axis, k):
        both = got_one.at[q, axis, k]
        return remote(both, both, one_s.at[q, axis, k], one_r.at[q, axis, k], along_x(k))

    halves = [half.at[q] for q in range(3)]
    gots = [got.at[q] for q in range(3)]

    def out_copy(n, axis, k, g, z):
        if axis == 0:
            at = lax.rem(y + k, SIDE)
            lon_at = x * (2 * SIDE) + at * 2 + z
        else:
            at = lax.rem(x + k, SIDE)
            lon_at = at * (2 * SIDE) + y * 2 + z
        src, dst = halves[n].at[axis, at, g, z], gots[n].at[k * RANKS + rank]
        return remote(src, dst, two_s.at[n], two_r.at[n], (2 * axis + g, lon_at))

    def own_copy(n, axis, g, z):
        src = halves[n].at[axis, y if axis == 0 else x, g, z]
        return pltpu.make_async_copy(src, gots[n].at[rank], two_r.at[n])

    def send_out(n, axis):
        rows = [(g, z) for g in range(2) for z in range(2)]
        for k in (2, 1, 3):
            for g, z in rows:
                out_copy(n, axis, k, g, z).start()
        for g, z in rows:
            here = (grp == 2 * axis + g) & (zh == z)

            @pl.when(here)
            def _():
                own_copy(n, axis, g, z).start()

            @pl.when(jnp.logical_not(here))
            def _():
                out_copy(n, axis, 0, g, z).start()

    def out_all(n):
        return remote(gots[n], gots[n], two_s.at[n], two_r.at[n], ring(1))

    def make_part(q, product):
        for g in (0, 2, 1, 3):
            part[q, g] = product(g).astype(bf16).reshape(SIDE, SIDE, 32, LANES)
            for k in (2, 1, 3):
                one_copy(q, k, g).start()

    def reduce_one(n, parts):
        for axis in range(2):
            for i, q in enumerate(parts):
                total = part[q, 0:2, x] if axis == 0 else part[q, 2:4, :, y]
                total = total.astype(f32)
                for k in range(1, SIDE):
                    one_pair(q, axis, k).wait_recv()
                    total = total + got_one[q, axis, k].astype(f32)
                total = total.astype(bf16).reshape(2, SIDE, 2, 16, LANES)
                for g in range(2):
                    half[n, axis, :, g, :, i] = total[g]
            send_out(n, axis)

    make_part(
        0,
        lambda g: lax.dot_general(
            second[:, g * 512 : g * 512 + 512], out_slope, TN, preferred_element_type=f32
        ),
    )

    for copy in in_copies:
        copy.wait_recv()

    def firsts_step(i, carry):
        c, n = lax.div(i, 2), lax.rem(i, 2)
        pre = lax.dot_general(
            wint[wide(c, BLOCK), :], inputs[wide(n, 512), :], NT, preferred_element_type=f32
        )
        firsts[wide(c, BLOCK), wide(n, 512)] = (pre * sigmoid(pre)).astype(bf16)
        return carry

    lax.fori_loop(0, 2 * RANKS, firsts_step, 0, unroll=2)

    for h in range(2):
        for k in range(1, RANKS):
            m_copy(k, h).wait_recv()
        make_part(
            1 + h,
            lambda g: jnp.dot(
                firsts[g * 512 : g * 512 + 512, :], mine[h], preferred_element_type=f32
            ),
        )
    reduce_one(0, (0,))
    for copy in in_copies + cnt_copies + halo_copies + sum_copies:
        copy.wait_send()
    for h in range(2):
        for k in range(1, RANKS):
            m_copy(k, h).wait_send()
    reduce_one(1, (1,))
    reduce_one(2, (2,))
    for q in range(3):
        for k in range(1, SIDE):
            for axis in range(2):
                one_pair(q, axis, k).wait_send()

    out_all(0).wait_recv()
    grad_out[...] = jnp.sum(got[0, :, 0].astype(f32), 0)
    for h in range(2):
        out_all(1 + h).wait_recv()
        total = jnp.sum(got[1 + h, :, 0].astype(f32).reshape(SIDE, RANKS, 16, LANES), 0)
        for t in range(RANKS):
            at = t * BLOCK + h * LANES
            grad_mid[:, at : at + LANES] = total[t]

    for n in range(3):
        sent = gots[n].at[1:]
        remote(sent, sent, two_s.at[n], two_r.at[n], ring(1)).wait_send()


def hand_on(a, b, c, a_out, b_out, c_out):
    a_out[...], b_out[...], c_out[...] = a[...], b[...], c[...]


def body(field, wind, w_in, w_mid, w_out, targets, column_map, batch_count):
    vmem = pl.BlockSpec(memory_space=pltpu.VMEM)
    hbm = pl.BlockSpec(memory_space=pltpu.HBM)
    hid = w_mid.shape[0]
    dma = pltpu.SemaphoreType.DMA
    V = pltpu.VMEM
    results = pl.pallas_call(
        kernel,
        out_shape=(
            jax.ShapeDtypeStruct((4, 32, LANES), f32),
            jax.ShapeDtypeStruct((16, hid), f32),
            jax.ShapeDtypeStruct((16, LANES), f32),
        ),
        in_specs=[hbm] * 8,
        out_specs=(vmem, vmem, vmem),
        scratch_shapes=[
            V((1, LANES), jnp.int32),
            V((1, 32), jnp.int32),
            V((2, 8, 48, LANES), f32),
            V((4, hid, WIDE), bf16),
            V((LANES, hid), bf16),
            V((hid, LANES), bf16),
            V((hid, LANES), bf16),
            V((LANES, LANES), f32),
            V((LANES, hid), bf16),
            V((hid, RANKS * LANES), bf16),
            V((LANES, hid), bf16),
            V((LANES, hid), f32),
            V((RANKS * LANES, LANES), bf16),
            V((6, 48, LANES), f32),
            V((2, RANKS, LANES, LANES), bf16),
            V((2, RANKS * LANES, LANES), bf16),
            V((8, LANES), f32),
            V((RANKS, 8, LANES), f32),
            V((8, LANES), f32),
            V((SIDE * SIDE, 8, LANES), f32),
            V((3, 4, SIDE, SIDE, 32, LANES), bf16),
            V((3, 2, SIDE, 2, SIDE, 32, LANES), bf16),
            V((3, 2, SIDE, 2, 2, 1, 16, LANES), bf16),
            V((3, SIDE * RANKS, 1, 16, LANES), bf16),
            dma((7,)),
            dma((4,)),
            dma((8,)),
            dma((8,)),
            dma((RANKS,)),
            dma((RANKS,)),
            dma((RANKS,)),
            dma((RANKS,)),
            dma((SIDE * SIDE,)),
            dma((SIDE * SIDE,)),
            dma((2, RANKS)),
            dma((2, RANKS)),
            dma((3, 2, SIDE)),
            dma((3, 2, SIDE)),
            dma((3,)),
            dma((3,)),
            pltpu.SemaphoreType.REGULAR((2,)),
        ],
        compiler_params=pltpu.CompilerParams(
            collective_id=0, has_side_effects=True, vmem_limit_bytes=VMEM_BYTES
        ),
        cost_estimate=pl.CostEstimate(
            flops=3_000_000_000, bytes_accessed=12_000_000, transcendentals=3_000_000
        ),
    )(
        field,
        wind,
        w_in,
        w_mid,
        w_out,
        targets,
        column_map.reshape(1, LANES),
        batch_count.reshape(1, 32),
    )
    return pl.pallas_call(
        hand_on,
        out_shape=tuple(jax.ShapeDtypeStruct(r.shape, r.dtype) for r in results),
        in_specs=[vmem] * 3,
        out_specs=(vmem,) * 3,
        compiler_params=pltpu.CompilerParams(vmem_limit_bytes=VMEM_BYTES),
    )(*results)


def solution(mesh):
    placed = (
        P("grp", "lon", None),
        P("grp", "lon", None),
        P(),
        P(),
        P(),
        P("lon", None),
        P("grp", "lon", None, None),
        P(),
    )
    return jax.shard_map(
        body,
        mesh=mesh,
        in_specs=placed,
        out_specs=(P("grp", "lon", None), P(("grp", "lon"), None), P(("grp", "lon"), None)),
        check_vma=False,
    )
```
